32 devices in a mesh: grp: 2 (over x), seq: 16 (over z, y, core).
Axes of the slice: x: 2, y: 2, z: 4, core: 2. Of those that a mesh axis runs over, the one named last changes fastest.
Arguments:
- scalars: bfloat16 [256, 4096], P(None, ('grp', 'seq')), parts along dimension 1, may hold values from -6 to 6
- vectors: bfloat16 [3, 256, 4096], P(None, None, ('grp', 'seq')), parts along dimension 2, may hold values from -6 to 6
- w_qkw_s: bfloat16 [2, 768, 256], replicated, may hold values from -0.375 to 0.375
- w_qkw_v: bfloat16 [2, 768, 256], replicated, may hold values from -0.375 to 0.375
- w_out_s: bfloat16 [2, 256, 256], replicated, may hold values from -0.375 to 0.375
- w_out_v: bfloat16 [2, 256, 256], replicated, may hold values from -0.375 to 0.375
- w_up: bfloat16 [2, 1024, 256], replicated, may hold values from -0.375 to 0.375
- w_down: bfloat16 [2, 256, 1024], replicated, may hold values from -0.1875 to 0.1875
- w_mix: bfloat16 [2, 256, 256], replicated, may hold values from -0.375 to 0.375
- w_gate: bfloat16 [2, 256, 256], replicated, may hold values from -0.375 to 0.375
- gains: float32 [2, 4, 256], replicated, may hold values from 0.5 to 1.5
- pe_w1: float32 [2, 64, 16], replicated, may hold values from -24 to 24
- pe_w2: float32 [2, 64, 64], replicated, may hold values from -0.75 to 0.75
- pe_w3: float32 [2, 256, 64], replicated, may hold values from -1.5 to 1.5
- rates: float32 [2, 256], replicated, may hold values from 0.05 to 40
Outputs:
- scalars_out: bfloat16 [256, 4096], P(None, ('grp', 'seq')), parts along dimension 1
- vectors_out: bfloat16 [3, 256, 4096], P(None, None, ('grp', 'seq')), parts along dimension 2
The draws below stay inside these ranges and needn't reach their ends.
There are 2 independent parts, one for each index of `grp`. The reference program is written for one: setup_inputs(seed, part) draws one part's arguments, and reference() takes and returns one part's arrays. A program takes and returns all parts, laid end to end along the dimension named above; an argument that names none is the same for every part. Nothing has to cross between parts.
All inputs are finite; a program needn't handle non-finite values.
Results may differ from the reference program's by a relative error of at most 0.02.
Values may be sent and summed in bfloat16 or wider, within the bound.
A program may use at most 64 MiB of HBM per device.

```python
import math
import jax
import jax.numpy as jnp
from jax import lax

CH = 256
FF = 1024
PEH = 64
PEF = 16
LAYERS = 2
TOKENS = 2048


def level_of(key, extent, pieces, low, high):
    factor_of, own = 1.0, jax.random.fold_in(key, 6)
    for position, blocks in pieces:
        draws = jnp.exp(jax.random.uniform(jax.random.fold_in(own, position), (blocks,), jnp.float32, low / len(pieces), high / len(pieces)))
        factor_of = factor_of * jnp.repeat(draws, extent[position] // blocks).reshape([-1 if axis == position else 1 for axis in range(len(extent))])
    return factor_of


def noise(key, extent, width, most, pieces=(), kind=jnp.bfloat16):
    result = width * jax.random.normal(key, extent, jnp.float32)
    if pieces:
        result = result * level_of(key, extent, pieces, -0.22, 0.18)
    return jnp.clip(result, -most, most).astype(kind)


def setup_inputs(seed: int = 0, part: int = 0) -> dict:
    splits = jax.random.split(jax.random.key(seed), 16)
    part_splits = jax.random.split(jax.random.fold_in(splits[15], part), 16)
    scalars = noise(part_splits[0], (CH, TOKENS), 1.0, 6.0, ((1, 16),))
    vectors = noise(part_splits[1], (3, CH, TOKENS), 1.0, 6.0, ((2, 16),))
    w_qkw_s = noise(splits[2], (LAYERS, 3 * CH, CH), CH ** -0.5, 0.375)
    w_qkw_v = noise(splits[3], (LAYERS, 3 * CH, CH), CH ** -0.5, 0.375)
    w_out_s = noise(splits[4], (LAYERS, CH, CH), CH ** -0.5, 0.375)
    w_out_v = noise(splits[5], (LAYERS, CH, CH), CH ** -0.5, 0.375)
    w_up = noise(splits[6], (LAYERS, FF, CH), CH ** -0.5, 0.375)
    w_down = noise(splits[7], (LAYERS, CH, FF), FF ** -0.5, 0.1875)
    w_mix = noise(splits[8], (LAYERS, CH, CH), CH ** -0.5, 0.375)
    w_gate = noise(splits[9], (LAYERS, CH, CH), CH ** -0.5, 0.375)
    gains = jnp.clip(1.0 + 0.1 * jax.random.normal(splits[10], (LAYERS, 4, CH), jnp.float32), 0.5, 1.5)
    pe_w1 = noise(splits[11], (LAYERS, PEH, PEF), 6.0, 24.0, (), jnp.float32)
    pe_w2 = noise(splits[12], (LAYERS, PEH, PEH), PEH ** -0.5, 0.75, (), jnp.float32)
    pe_w3 = noise(splits[13], (LAYERS, CH, PEH), (PEH // 4) ** -0.5, 1.5, (), jnp.float32)
    rates = jnp.clip(jnp.exp(jax.random.uniform(splits[14], (LAYERS, CH), jnp.float32, math.log(0.05), math.log(40.0))), 0.05, 40.0)
    return {"scalars": scalars, "vectors": vectors, "w_qkw_s": w_qkw_s, "w_qkw_v": w_qkw_v, "w_out_s": w_out_s, "w_out_v": w_out_v, "w_up": w_up, "w_down": w_down, "w_mix": w_mix, "w_gate": w_gate, "gains": gains, "pe_w1": pe_w1, "pe_w2": pe_w2, "pe_w3": pe_w3, "rates": rates}


def filter_values(positions, length, first, second, third, decay):
    count = first.shape[1] // 2
    freqs = jnp.arange(1, count + 1, dtype=jnp.int32)
    turns = freqs[:, None] * positions[None, :] % length
    angle = turns.astype(jnp.float32) * (2.0 * math.pi / length)
    feats = jnp.concatenate([jnp.cos(angle), jnp.sin(angle)], axis=0)
    hid_one = jnp.sin(jnp.dot(first, feats, precision=lax.Precision.HIGHEST))
    hid_two = jnp.sin(jnp.dot(second, hid_one, precision=lax.Precision.HIGHEST))
    raw = jnp.dot(third, hid_two, precision=lax.Precision.HIGHEST)
    envelope = jnp.exp(-decay[:, None] * positions[None, :].astype(jnp.float32) / length)
    return (raw * envelope / math.sqrt(length)).astype(jnp.bfloat16)

def scalar_norm(field, gain):
    return field * lax.rsqrt(lax.optimization_barrier(jnp.mean(field * field, axis=0, keepdims=True)) + 1e-05) * gain[:, None]

def vector_norm(field, gain):
    return field * lax.rsqrt(lax.optimization_barrier(jnp.mean(field * field, axis=(0, 1), keepdims=True)) + 1e-05) * gain[None, :, None]

def mix_vec(weight, field):
    return jnp.einsum('oc,jct->jot', weight.astype(jnp.float32), field.astype(jnp.float32))

def reference(scalars, vectors, w_qkw_s, w_qkw_v, w_out_s, w_out_v, w_up, w_down, w_mix, w_gate, gains, pe_w1, pe_w2, pe_w3, rates):
    length = scalars.shape[1]
    chans = scalars.shape[0]
    positions = jnp.arange(length, dtype=jnp.int32)
    state_s = scalars.astype(jnp.float32)
    state_v = vectors.astype(jnp.float32)
    for layer in range(w_qkw_s.shape[0]):
        filt = filter_values(positions, length, pe_w1[layer], pe_w2[layer], pe_w3[layer], rates[layer])
        normed_s = scalar_norm(state_s, gains[layer, 0]).astype(jnp.bfloat16)
        normed_v = vector_norm(state_v, gains[layer, 1]).astype(jnp.bfloat16)
        proj_s = jnp.dot(w_qkw_s[layer], normed_s, preferred_element_type=jnp.float32)
        query_s = proj_s[:chans].astype(jnp.bfloat16)
        signal_s = (proj_s[chans:2 * chans] * proj_s[2 * chans:]).astype(jnp.bfloat16)
        proj_v = mix_vec(w_qkw_v[layer], normed_v)
        query_v = proj_v[:, :chans].astype(jnp.bfloat16)
        key_v = proj_v[:, chans:2 * chans].astype(jnp.bfloat16)
        value_v = proj_v[:, 2 * chans:].astype(jnp.bfloat16)
        spec_h = jnp.fft.fft(filt.astype(jnp.float32), axis=-1)
        spec_x = jnp.fft.fft(signal_s.astype(jnp.float32), axis=-1)
        conv_s = jnp.real(jnp.fft.ifft(spec_h * spec_x, axis=-1)).astype(jnp.float32).astype(jnp.bfloat16)
        spec_k = jnp.fft.fft(key_v.astype(jnp.float32), axis=-1)
        spec_w = jnp.fft.fft(value_v.astype(jnp.float32), axis=-1)
        k_one = jnp.roll(spec_k, -1, axis=0)
        k_two = jnp.roll(spec_k, -2, axis=0)
        w_one = jnp.roll(spec_w, -1, axis=0)
        w_two = jnp.roll(spec_w, -2, axis=0)
        cross = k_one * w_two - k_two * w_one
        conv_v = (jnp.real(jnp.fft.ifft(cross, axis=-1)).astype(jnp.float32) / math.sqrt(length)).astype(jnp.bfloat16)
        qs_f = query_s.astype(jnp.float32)
        out_s = (qs_f * conv_s.astype(jnp.float32) + lax.optimization_barrier(jnp.sum(query_v.astype(jnp.float32) * conv_v.astype(jnp.float32), axis=0))).astype(jnp.bfloat16)
        out_v = (qs_f[None] * conv_v.astype(jnp.float32)).astype(jnp.bfloat16)
        state_s = state_s + jnp.dot(w_out_s[layer], out_s, preferred_element_type=jnp.float32)
        state_v = state_v + mix_vec(w_out_v[layer], out_v)
        mlp_s = scalar_norm(state_s, gains[layer, 2]).astype(jnp.bfloat16)
        mlp_v = vector_norm(state_v, gains[layer, 3]).astype(jnp.bfloat16)
        hidden = jax.nn.gelu(jnp.dot(w_up[layer], mlp_s, preferred_element_type=jnp.float32)).astype(jnp.bfloat16)
        gate = jax.nn.sigmoid(jnp.dot(w_gate[layer], mlp_s, preferred_element_type=jnp.float32))
        state_s = state_s + jnp.dot(w_down[layer], hidden, preferred_element_type=jnp.float32)
        state_v = state_v + mix_vec(w_mix[layer], mlp_v) * gate[None]
    return (state_s.astype(jnp.bfloat16), state_v.astype(jnp.bfloat16))
```

```python
import functools
import math

import jax
import jax.numpy as jnp
import numpy as np
from jax import lax
from jax.experimental import pallas as pl
from jax.experimental.pallas import tpu as pltpu
from jax.sharding import PartitionSpec as P


def filter_values(positions, length, first, second, third, decay):
    count = first.shape[1] // 2
    freqs = jnp.arange(1, count + 1, dtype=jnp.int32)
    turns = freqs[:, None] * positions[None, :] % length
    angle = turns.astype(jnp.float32) * (2.0 * math.pi / length)
    feats = jnp.concatenate([jnp.cos(angle), jnp.sin(angle)], axis=0)
    hid_one = jnp.sin(jnp.dot(first, feats, precision=lax.Precision.HIGHEST))
    hid_two = jnp.sin(jnp.dot(second, hid_one, precision=lax.Precision.HIGHEST))
    raw = jnp.dot(third, hid_two, precision=lax.Precision.HIGHEST)
    envelope = jnp.exp(-decay[:, None] * positions[None, :].astype(jnp.float32) / length)
    return (raw * envelope / math.sqrt(length)).astype(jnp.bfloat16)


def scalar_norm(field, gain):
    return field * lax.rsqrt(jnp.mean(field * field, axis=0, keepdims=True) + 1e-05) * gain[:, None]


def vector_norm(field, gain):
    return (
        field
        * lax.rsqrt(jnp.mean(field * field, axis=(0, 1), keepdims=True) + 1e-05)
        * gain[None, :, None]
    )


def square_table(count):
    index = jnp.arange(count, dtype=jnp.int32)
    turns = index[:, None] * index[None, :] % count
    angle = turns.astype(jnp.float32) * (2.0 * math.pi / count)
    return (jnp.cos(angle), jnp.sin(angle))


def make_tables(length):
    side_b = 1
    for candidate in range(1, math.isqrt(length) + 1):
        if length % candidate == 0:
            side_b = candidate
    side_a = length // side_b
    cos_b, sin_b = square_table(side_b)
    cos_a, sin_a = square_table(side_a)
    rows_b = jnp.arange(side_b, dtype=jnp.int32)
    cols_a = jnp.arange(side_a, dtype=jnp.int32)
    angle = (rows_b[:, None] * cols_a[None, :]).astype(jnp.float32) * (2.0 * math.pi / length)
    return (side_b, side_a, cos_b, sin_b, cos_a, sin_a, jnp.cos(angle), jnp.sin(angle))


def forward_dft(signal, tables):
    side_b, side_a, cos_b, sin_b, cos_a, sin_a, twist_r, twist_s = tables
    high = lax.Precision.HIGHEST
    first_r = jnp.einsum("cb,...ba->...ca", cos_b, signal, precision=high)
    first_i = -jnp.einsum("cb,...ba->...ca", sin_b, signal, precision=high)
    mid_r = first_r * twist_r + first_i * twist_s
    mid_i = first_i * twist_r - first_r * twist_s
    out_r = jnp.einsum("...ca,ad->...cd", mid_r, cos_a, precision=high) + jnp.einsum(
        "...ca,ad->...cd", mid_i, sin_a, precision=high
    )
    out_i = jnp.einsum("...ca,ad->...cd", mid_i, cos_a, precision=high) - jnp.einsum(
        "...ca,ad->...cd", mid_r, sin_a, precision=high
    )
    return (out_r, out_i)


def inverse_dft(spec_r, spec_i, tables):
    side_b, side_a, cos_b, sin_b, cos_a, sin_a, twist_r, twist_s = tables
    high = lax.Precision.HIGHEST
    back_r = jnp.einsum("...cd,da->...ca", spec_r, cos_a, precision=high) - jnp.einsum(
        "...cd,da->...ca", spec_i, sin_a, precision=high
    )
    back_i = jnp.einsum("...cd,da->...ca", spec_i, cos_a, precision=high) + jnp.einsum(
        "...cd,da->...ca", spec_r, sin_a, precision=high
    )
    turn_r = back_r * twist_r - back_i * twist_s
    turn_i = back_i * twist_r + back_r * twist_s
    whole = jnp.einsum("bc,...ca->...ba", cos_b, turn_r, precision=high) - jnp.einsum(
        "bc,...ca->...ba", sin_b, turn_i, precision=high
    )
    return whole / (side_b * side_a)


def convolve(fields, filt, tables):
    side_b, side_a = (tables[0], tables[1])
    length = side_b * side_a
    chans = fields.shape[1]
    stacked = jnp.concatenate([fields[0:1], filt[None], fields[1:]], axis=0).astype(jnp.float32)
    spec_r, spec_i = forward_dft(stacked.reshape(8, chans, side_b, side_a), tables)
    prod_r = spec_r[0] * spec_r[1] - spec_i[0] * spec_i[1]
    prod_i = spec_r[0] * spec_i[1] + spec_i[0] * spec_r[1]
    key_r, key_i = (spec_r[2:5], spec_i[2:5])
    val_r, val_i = (spec_r[5:8], spec_i[5:8])
    k_one_r, k_one_i = (jnp.roll(key_r, -1, axis=0), jnp.roll(key_i, -1, axis=0))
    k_two_r, k_two_i = (jnp.roll(key_r, -2, axis=0), jnp.roll(key_i, -2, axis=0))
    v_one_r, v_one_i = (jnp.roll(val_r, -1, axis=0), jnp.roll(val_i, -1, axis=0))
    v_two_r, v_two_i = (jnp.roll(val_r, -2, axis=0), jnp.roll(val_i, -2, axis=0))
    cross_r = k_one_r * v_two_r - k_one_i * v_two_i - (k_two_r * v_one_r - k_two_i * v_one_i)
    cross_i = k_one_r * v_two_i + k_one_i * v_two_r - (k_two_r * v_one_i + k_two_i * v_one_r)
    all_r = jnp.concatenate([prod_r[None], cross_r], axis=0)
    all_i = jnp.concatenate([prod_i[None], cross_i], axis=0)
    result = inverse_dft(all_r, all_i, tables).reshape(4, chans, length)
    inv_root = 1.0 / math.sqrt(length)
    scale = jnp.array([1.0, inv_root, inv_root, inv_root], dtype=jnp.float32)
    return (result * scale[:, None, None]).astype(jnp.bfloat16)


def plain_device(
    scalars,
    vectors,
    w_qkw_s,
    w_qkw_v,
    w_out_s,
    w_out_v,
    w_up,
    w_down,
    w_mix,
    w_gate,
    gains,
    pe_w1,
    pe_w2,
    pe_w3,
    rates,
):
    chans = scalars.shape[0]
    tok_local = scalars.shape[1]
    shards = lax.axis_size("seq")
    rank = lax.axis_index("seq")
    length = tok_local * shards
    depth = w_qkw_s.shape[0]
    tables = make_tables(length)
    local_pos = rank * tok_local + jnp.arange(tok_local, dtype=jnp.int32)
    made = jnp.stack(
        [
            filter_values(local_pos, length, pe_w1[layer], pe_w2[layer], pe_w3[layer], rates[layer])
            for layer in range(depth)
        ],
        axis=0,
    )
    filters = lax.all_to_all(made, "seq", split_axis=1, concat_axis=2, tiled=True)
    state_s = scalars.astype(jnp.float32)
    state_v = vectors.astype(jnp.float32)
    for layer in range(depth):
        normed_s = scalar_norm(state_s, gains[layer, 0]).astype(jnp.bfloat16)
        normed_v = vector_norm(state_v, gains[layer, 1]).astype(jnp.bfloat16)
        proj_s = jnp.dot(w_qkw_s[layer], normed_s, preferred_element_type=jnp.float32)
        query_s = proj_s[:chans].astype(jnp.bfloat16)
        signal_s = (proj_s[chans : 2 * chans] * proj_s[2 * chans :]).astype(jnp.bfloat16)
        proj_v = jnp.einsum(
            "oc,jct->jot", w_qkw_v[layer], normed_v, preferred_element_type=jnp.float32
        ).astype(jnp.bfloat16)
        query_v = proj_v[:, :chans]
        outgoing = jnp.concatenate(
            [signal_s[None], proj_v[:, chans : 2 * chans], proj_v[:, 2 * chans :]], axis=0
        )
        regrouped = lax.all_to_all(outgoing, "seq", split_axis=1, concat_axis=2, tiled=True)
        convolved = convolve(regrouped, filters[layer], tables)
        returned = lax.all_to_all(convolved, "seq", split_axis=2, concat_axis=1, tiled=True)
        conv_f = returned.astype(jnp.float32)
        qs_f = query_s.astype(jnp.float32)
        out_s = (
            qs_f * conv_f[0] + jnp.sum(query_v.astype(jnp.float32) * conv_f[1:], axis=0)
        ).astype(jnp.bfloat16)
        out_v = (qs_f[None] * conv_f[1:]).astype(jnp.bfloat16)
        state_s = state_s + jnp.dot(w_out_s[layer], out_s, preferred_element_type=jnp.float32)
        state_v = state_v + jnp.einsum(
            "oc,jct->jot", w_out_v[layer], out_v, preferred_element_type=jnp.float32
        )
        mlp_s = scalar_norm(state_s, gains[layer, 2]).astype(jnp.bfloat16)
        mlp_v = vector_norm(state_v, gains[layer, 3]).astype(jnp.bfloat16)
        hidden = jax.nn.gelu(
            jnp.dot(w_up[layer], mlp_s, preferred_element_type=jnp.float32)
        ).astype(jnp.bfloat16)
        gate = jax.nn.sigmoid(jnp.dot(w_gate[layer], mlp_s, preferred_element_type=jnp.float32))
        state_s = state_s + jnp.dot(w_down[layer], hidden, preferred_element_type=jnp.float32)
        state_v = (
            state_v
            + jnp.einsum("oc,jct->jot", w_mix[layer], mlp_v, preferred_element_type=jnp.float32)
            * gate[None]
        )
    return (state_s.astype(jnp.bfloat16), state_v.astype(jnp.bfloat16))


def reduced_sine(angle):
    turns = jnp.floor(angle * (1.0 / math.pi) + 0.5)
    rest = angle - turns * 3.140625
    rest = rest - turns * 9.67502593994140625e-4
    rest = rest - turns * 1.509957990978376432e-7
    half = turns * 0.5
    sign = 1.0 - 4.0 * (half - jnp.floor(half))
    sq = rest * rest
    poly = -2.5052108e-8
    poly = poly * sq + 2.7557319e-6
    poly = poly * sq - 1.9841270e-4
    poly = poly * sq + 8.3333333e-3
    poly = poly * sq - 1.6666667e-1
    return sign * (rest + rest * sq * poly)


def part_sum(one, two):
    if one is None:
        return two
    if two is None:
        return one
    return one + two


def part_diff(one, two):
    if two is None:
        return one
    if one is None:
        return -two
    return one - two


def turn(value, step, count):
    step = step % count
    real, imag = value
    if step == 0:
        return value
    if 4 * step == count:
        return (None if imag is None else -imag, real)
    if 4 * step == 3 * count:
        return (imag, None if real is None else -real)
    cos, sin = (math.cos(2 * math.pi * step / count), math.sin(2 * math.pi * step / count))
    if imag is None:
        return (real * cos, real * sin)
    if real is None:
        return (imag * -sin, imag * cos)
    return (real * cos - imag * sin, imag * cos + real * sin)


def real_fft(fields):
    count = len(fields)
    if count == 1:
        return [(fields[0], None)]
    if count == 2:
        return [(fields[0] + fields[1], None), (fields[0] - fields[1], None)]
    even, odd = (real_fft(fields[0::2]), real_fft(fields[1::2]))
    out = [None] * (count // 2 + 1)
    for k in range(count // 4 + 1):
        spun = turn(odd[k], -k, count)
        out[k] = (part_sum(even[k][0], spun[0]), part_sum(even[k][1], spun[1]))
        back = (part_diff(even[k][0], spun[0]), part_diff(spun[1], even[k][1]))
        if count // 2 - k != k:
            out[count // 2 - k] = back
    return out


def inverse_real_fft(spec, count):
    if count == 1:
        return [spec[0][0]]
    if count == 2:
        return [spec[0][0] + spec[1][0], spec[0][0] - spec[1][0]]
    even, odd = ([], [])
    for k in range(count // 4 + 1):
        one, two = (spec[k], spec[count // 2 - k])
        if 4 * k == count:
            even.append((one[0] * 2.0, None))
            odd.append((one[1] * -2.0, None))
            continue
        even.append((part_sum(one[0], two[0]), part_diff(one[1], two[1])))
        diff = (part_diff(one[0], two[0]), part_sum(one[1], two[1]))
        odd.append(turn(diff, k, count))
    out = [None] * count
    out[0::2] = inverse_real_fft(even, count // 2)
    out[1::2] = inverse_real_fft(odd, count // 2)
    return out


def local_tables(shards, tok_local):
    length = shards * tok_local
    freq = np.arange(shards // 2 + 1)[:, None, None] + shards * np.arange(tok_local)[None, None, :]
    angle = (np.arange(tok_local)[None, :, None] * freq % length) * (2.0 * np.pi / length)
    cos, sin = (np.cos(angle), np.sin(angle))
    fore = np.concatenate(
        [np.concatenate([cos, -sin], axis=2), np.concatenate([sin, cos], axis=2)], axis=1
    )
    cos, sin = (cos.transpose(0, 2, 1), sin.transpose(0, 2, 1))
    back = np.concatenate(
        [np.concatenate([cos, sin], axis=2), np.concatenate([-sin, cos], axis=2)], axis=1
    )
    return (jnp.asarray(fore, jnp.bfloat16), jnp.asarray(back / length, jnp.bfloat16))


def layers_kernel(
    shards,
    scalars,
    vectors,
    w_qkw_s,
    w_qkw_v,
    w_out_s,
    w_out_v,
    w_up,
    w_down,
    w_mix,
    w_gate,
    gains,
    pe_w1,
    pe_w2,
    pe_w3,
    rates,
    fore,
    back,
    scalars_out,
    vectors_out,
    state_s,
    state_v,
    query_s,
    query_v,
    sent_f,
    got_f,
    sent_x,
    got_x,
    sent_y,
    got_y,
    mid,
    inv,
    send_sem,
    recv_sem,
):
    grp = lax.axis_index("grp")
    me = lax.axis_index("seq")
    chans, tok = scalars.shape
    own = chans // shards
    length = shards * tok
    depth = w_qkw_s.shape[0]
    half = shards // 2 + 1
    f32, bf16 = (jnp.float32, jnp.bfloat16)
    mesh_id = pl.DeviceIdType.MESH

    barrier = pltpu.get_barrier_semaphore()

    def greet(step, carry):
        peer = lax.rem(me + step, shards)
        pl.semaphore_signal(barrier, inc=1, device_id=(grp, peer), device_id_type=mesh_id)
        return carry

    lax.fori_loop(1, shards, greet, 0)

    def copy_of(kind, src, dst, peer, lane):
        return pltpu.make_async_remote_copy(
            src_ref=src,
            dst_ref=dst,
            send_sem=send_sem.at[kind, peer],
            recv_sem=recv_sem.at[kind, lane],
            device_id=(grp, peer),
            device_id_type=mesh_id,
        )

    def send(kind, src, dst, rows):
        def body(step, carry):
            peer = lax.rem(me + step, shards)
            copy_of(kind, src.at[peer, rows], dst.at[me, rows], peer, me).start()
            return carry

        lax.fori_loop(1, shards, body, 0)
        dst[pl.ds(me, 1), rows] = src[pl.ds(me, 1), rows]

    def receive(kind, dst, rows):
        def body(step, carry):
            peer = lax.rem(me + step, shards)
            copy_of(kind, dst.at[peer, rows], dst.at[peer, rows], peer, peer).wait_recv()
            return carry

        lax.fori_loop(1, shards, body, 0)

    def sent(kind, src, rows):
        def body(step, carry):
            peer = lax.rem(me + step, shards)
            copy_of(kind, src.at[peer, rows], src.at[peer, rows], peer, peer).wait_send()
            return carry

        lax.fori_loop(1, shards, body, 0)

    def column(row):
        return jnp.broadcast_to(row, (tok, chans)).T

    def normed_scalar(field, gain):
        return (
            field * lax.rsqrt(jnp.mean(field * field, axis=0, keepdims=True) + 1e-05) * gain
        ).astype(bf16)

    def normed_vector(fields, gain):
        total = sum(jnp.sum(field * field, axis=0, keepdims=True) for field in fields)
        scale = lax.rsqrt(total * (1.0 / (3 * chans)) + 1e-05)
        return jnp.concatenate([(field * scale * gain).astype(bf16) for field in fields], axis=1)

    def make_filter(layer):
        count = pe_w1.shape[2] // 2
        row = lax.broadcasted_iota(jnp.int32, (2 * count, tok), 0)
        pos = me * tok + lax.broadcasted_iota(jnp.int32, (2 * count, tok), 1)
        is_cos = row < count
        turns = (jnp.where(is_cos, row + 1, row + 1 - count) * pos).astype(f32)
        turns = turns + jnp.where(is_cos, length / 4.0, 0.0)
        turns = turns - length * jnp.floor(turns * (1.0 / length))
        feats = reduced_sine(turns * (2.0 * math.pi / length))
        high = lax.Precision.HIGHEST
        one = reduced_sine(jnp.dot(pe_w1[layer], feats, precision=high, preferred_element_type=f32))
        two = reduced_sine(jnp.dot(pe_w2[layer], one, precision=high, preferred_element_type=f32))
        raw = jnp.dot(pe_w3[layer], two, precision=high, preferred_element_type=f32)
        place = (me * tok + lax.broadcasted_iota(jnp.int32, (chans, tok), 1)).astype(f32)
        rate = column(rates[pl.ds(layer, 1), :])
        made = raw * jnp.exp(-rate * place * (1.0 / length)) * (1.0 / math.sqrt(length))
        sent_f[:, layer * own : (layer + 1) * own, :] = made.astype(bf16).reshape(shards, own, tok)

    def spread(fields, row):
        spec = real_fft(fields)
        for k in range(half):
            real, imag = spec[k]
            mid[k, row : row + own, 0:tok] = real.astype(bf16)
            if imag is None:
                imag = jnp.zeros_like(real)
            mid[k, row : row + own, tok : 2 * tok] = imag.astype(bf16)

    def gather_back(layer, signal, scale):
        spec = []
        for k in range(half):
            imag = None if k in (0, half - 1) else inv[k, signal * own : (signal + 1) * own, tok : 2 * tok]
            spec.append((inv[k, signal * own : (signal + 1) * own, 0:tok], imag))
        out = inverse_real_fft(spec, shards)
        for r in range(shards):
            value = out[r] if scale is None else out[r] * scale
            sent_y[layer, r, signal * own : (signal + 1) * own, :] = value.astype(bf16)

    def incoming(ref, row):
        return [ref[r, row : row + own, :].astype(f32) for r in range(shards)]

    def times(one, two):
        return (one[0] * two[0] - one[1] * two[1], one[0] * two[1] + one[1] * two[0])

    state_s[...] = scalars[...].astype(f32)
    state_v[...] = vectors[...].astype(f32)
    vec_rows, sca_rows = (pl.ds(0, 6 * own), pl.ds(6 * own, own))
    for layer in range(depth):
        base = 4 * layer
        fields = [state_v[j] for j in range(3)]
        vn = normed_vector(fields, column(gains[layer, 1:2, :]))
        pv = jnp.dot(w_qkw_v[layer, chans:, :], vn, preferred_element_type=f32).astype(bf16)
        for j in range(3):
            cols = slice(j * tok, (j + 1) * tok)
            sent_x[layer, :, j * own : (j + 1) * own, :] = pv[:chans, cols].reshape(shards, own, tok)
            sent_x[layer, :, (3 + j) * own : (4 + j) * own, :] = pv[chans:, cols].reshape(
                shards, own, tok
            )
        if layer == 0:
            pl.semaphore_wait(barrier, shards - 1)
        send(base, sent_x.at[layer], got_x.at[layer], vec_rows)
        sn = normed_scalar(state_s[...], column(gains[layer, 0:1, :]))
        ps = jnp.dot(w_qkw_s[layer, chans:, :], sn, preferred_element_type=f32)
        sent_x[layer, :, 6 * own : 7 * own, :] = (
            (ps[:chans] * ps[chans:]).astype(bf16).reshape(shards, own, tok)
        )
        send(base + 1, sent_x.at[layer], got_x.at[layer], sca_rows)
        if layer == 0:
            for each in range(depth):
                make_filter(each)
            send(4 * depth, sent_f, got_f, pl.ds(0, depth * own))
        query_s[...] = jnp.dot(w_qkw_s[layer, :chans, :], sn, preferred_element_type=f32).astype(bf16)
        query_v[...] = jnp.dot(w_qkw_v[layer, :chans, :], vn, preferred_element_type=f32).astype(bf16)

        receive(base, got_x.at[layer], vec_rows)
        for signal in range(6):
            spread(incoming(got_x.at[layer], signal * own), signal * own)
        for k in range(half):
            spec = jnp.dot(mid[k, : 6 * own, :], fore[k], preferred_element_type=f32)
            parts = [
                (spec[i * own : (i + 1) * own, :tok], spec[i * own : (i + 1) * own, tok:])
                for i in range(6)
            ]
            rows = []
            for j in range(3):
                plus = times(parts[(j + 1) % 3], parts[3 + (j + 2) % 3])
                minus = times(parts[(j + 2) % 3], parts[3 + (j + 1) % 3])
                rows.append(jnp.concatenate([plus[0] - minus[0], plus[1] - minus[1]], axis=1))
            inv[k, : 3 * own, :] = jnp.dot(
                jnp.concatenate(rows, axis=0).astype(bf16), back[k], preferred_element_type=f32
            )
        for signal in range(3):
            gather_back(layer, signal, 1.0 / math.sqrt(length))
        send(base + 2, sent_y.at[layer], got_y.at[layer], pl.ds(0, 3 * own))

        receive(base + 1, got_x.at[layer], sca_rows)
        if layer == 0:
            receive(4 * depth, got_f, pl.ds(0, depth * own))
        spread(incoming(got_x.at[layer], 6 * own), 6 * own)
        spread(incoming(got_f, layer * own), 7 * own)
        for k in range(half):
            spec = jnp.dot(mid[k, 6 * own :, :], fore[k], preferred_element_type=f32)
            prod = times((spec[:own, :tok], spec[:own, tok:]), (spec[own:, :tok], spec[own:, tok:]))
            inv[k, 3 * own :, :] = jnp.dot(
                jnp.concatenate(prod, axis=1).astype(bf16), back[k], preferred_element_type=f32
            )
        gather_back(layer, 3, None)
        send(base + 3, sent_y.at[layer], got_y.at[layer], pl.ds(3 * own, own))

        receive(base + 2, got_y.at[layer], pl.ds(0, 3 * own))
        qs = query_s[...].astype(f32)
        out_v = []
        mixed = None
        for j in range(3):
            field = got_y[layer, :, j * own : (j + 1) * own, :].reshape(chans, tok).astype(f32)
            term = query_v[:, j * tok : (j + 1) * tok].astype(f32) * field
            mixed = term if mixed is None else mixed + term
            out_v.append((qs * field).astype(bf16))
        moved = jnp.dot(w_out_v[layer], jnp.concatenate(out_v, axis=1), preferred_element_type=f32)
        fields = [state_v[j] + moved[:, j * tok : (j + 1) * tok] for j in range(3)]
        vm = normed_vector(fields, column(gains[layer, 3:4, :]))
        mix = jnp.dot(w_mix[layer], vm, preferred_element_type=f32)
        receive(base + 3, got_y.at[layer], pl.ds(3 * own, own))
        field = got_y[layer, :, 3 * own : 4 * own, :].reshape(chans, tok).astype(f32)
        out_s = (qs * field + mixed).astype(bf16)
        now_s = state_s[...] + jnp.dot(w_out_s[layer], out_s, preferred_element_type=f32)
        sm = normed_scalar(now_s, column(gains[layer, 2:3, :]))
        hidden = jax.nn.gelu(jnp.dot(w_up[layer], sm, preferred_element_type=f32)).astype(bf16)
        gate = jax.nn.sigmoid(jnp.dot(w_gate[layer], sm, preferred_element_type=f32))
        now_s = now_s + jnp.dot(w_down[layer], hidden, preferred_element_type=f32)
        now_v = [fields[j] + mix[:, j * tok : (j + 1) * tok] * gate for j in range(3)]
        if layer + 1 < depth:
            state_s[...] = now_s
            for j in range(3):
                state_v[j] = now_v[j]
        else:
            scalars_out[...] = now_s.astype(bf16)
            for j in range(3):
                vectors_out[j] = now_v[j].astype(bf16)
    for layer in range(depth):
        base = 4 * layer
        sent(base, sent_x.at[layer], vec_rows)
        sent(base + 1, sent_x.at[layer], sca_rows)
        sent(base + 2, sent_y.at[layer], pl.ds(0, 3 * own))
        sent(base + 3, sent_y.at[layer], pl.ds(3 * own, own))
    sent(4 * depth, sent_f, pl.ds(0, depth * own))


def per_device(*arrays):
    scalars, vectors, w_qkw_s = arrays[:3]
    chans, tok = scalars.shape
    shards = lax.axis_size("seq")
    depth = w_qkw_s.shape[0]
    own = chans // shards
    if tok % 128 or own % 16 or chans % shards or shards & (shards - 1) or shards < 4:
        return plain_device(*arrays)
    half = shards // 2 + 1
    fore, back = local_tables(shards, tok)
    f32, bf16 = (jnp.float32, jnp.bfloat16)
    whole = pl.BlockSpec(memory_space=pltpu.VMEM)
    return pl.pallas_call(
        functools.partial(layers_kernel, shards),
        out_shape=(
            jax.ShapeDtypeStruct(scalars.shape, bf16),
            jax.ShapeDtypeStruct(vectors.shape, bf16),
        ),
        in_specs=[whole] * (len(arrays) + 2),
        out_specs=(whole, whole),
        scratch_shapes=[
            pltpu.VMEM((chans, tok), f32),
            pltpu.VMEM((3, chans, tok), f32),
            pltpu.VMEM((chans, tok), bf16),
            pltpu.VMEM((chans, 3 * tok), bf16),
            pltpu.VMEM((shards, depth * own, tok), bf16),
            pltpu.VMEM((shards, depth * own, tok), bf16),
            pltpu.VMEM((depth, shards, 7 * own, tok), bf16),
            pltpu.VMEM((depth, shards, 7 * own, tok), bf16),
            pltpu.VMEM((depth, shards, 4 * own, tok), bf16),
            pltpu.VMEM((depth, shards, 4 * own, tok), bf16),
            pltpu.VMEM((half, 8 * own, 2 * tok), bf16),
            pltpu.VMEM((half, 4 * own, 2 * tok), f32),
            pltpu.SemaphoreType.DMA((4 * depth + 1, shards)),
            pltpu.SemaphoreType.DMA((4 * depth + 1, shards)),
        ],
        compiler_params=pltpu.CompilerParams(
            collective_id=0, has_side_effects=True, vmem_limit_bytes=40 * 1024 * 1024
        ),
        name="hyena_layers",
    )(*arrays, fore, back)


def solution(mesh):
    in_specs = (
        P(None, ("grp", "seq")),
        P(None, None, ("grp", "seq")),
        P(),
        P(),
        P(),
        P(),
        P(),
        P(),
        P(),
        P(),
        P(),
        P(),
        P(),
        P(),
        P(),
    )
    out_specs = (P(None, ("grp", "seq")), P(None, None, ("grp", "seq")))
    return jax.shard_map(
        per_device, mesh=mesh, in_specs=in_specs, out_specs=out_specs, check_vma=False
    )
```

```python
import functools
import math

import jax
import jax.numpy as jnp
import numpy as np
from jax import lax
from jax.experimental import pallas as pl
from jax.experimental.pallas import tpu as pltpu
from jax.sharding import PartitionSpec as P


def filter_values(positions, length, first, second, third, decay):
    count = first.shape[1] // 2
    freqs = jnp.arange(1, count + 1, dtype=jnp.int32)
    turns = freqs[:, None] * positions[None, :] % length
    angle = turns.astype(jnp.float32) * (2.0 * math.pi / length)
    feats = jnp.concatenate([jnp.cos(angle), jnp.sin(angle)], axis=0)
    hid_one = jnp.sin(jnp.dot(first, feats, precision=lax.Precision.HIGHEST))
    hid_two = jnp.sin(jnp.dot(second, hid_one, precision=lax.Precision.HIGHEST))
    raw = jnp.dot(third, hid_two, precision=lax.Precision.HIGHEST)
    envelope = jnp.exp(-decay[:, None] * positions[None, :].astype(jnp.float32) / length)
    return (raw * envelope / math.sqrt(length)).astype(jnp.bfloat16)


def scalar_norm(field, gain):
    return field * lax.rsqrt(jnp.mean(field * field, axis=0, keepdims=True) + 1e-05) * gain[:, None]


def vector_norm(field, gain):
    return (
        field
        * lax.rsqrt(jnp.mean(field * field, axis=(0, 1), keepdims=True) + 1e-05)
        * gain[None, :, None]
    )


def square_table(count):
    index = jnp.arange(count, dtype=jnp.int32)
    turns = index[:, None] * index[None, :] % count
    angle = turns.astype(jnp.float32) * (2.0 * math.pi / count)
    return (jnp.cos(angle), jnp.sin(angle))


def make_tables(length):
    side_b = 1
    for candidate in range(1, math.isqrt(length) + 1):
        if length % candidate == 0:
            side_b = candidate
    side_a = length // side_b
    cos_b, sin_b = square_table(side_b)
    cos_a, sin_a = square_table(side_a)
    rows_b = jnp.arange(side_b, dtype=jnp.int32)
    cols_a = jnp.arange(side_a, dtype=jnp.int32)
    angle = (rows_b[:, None] * cols_a[None, :]).astype(jnp.float32) * (2.0 * math.pi / length)
    return (side_b, side_a, cos_b, sin_b, cos_a, sin_a, jnp.cos(angle), jnp.sin(angle))


def forward_dft(signal, tables):
    side_b, side_a, cos_b, sin_b, cos_a, sin_a, twist_r, twist_s = tables
    high = lax.Precision.HIGHEST
    first_r = jnp.einsum("cb,...ba->...ca", cos_b, signal, precision=high)
    first_i = -jnp.einsum("cb,...ba->...ca", sin_b, signal, precision=high)
    mid_r = first_r * twist_r + first_i * twist_s
    mid_i = first_i * twist_r - first_r * twist_s
    out_r = jnp.einsum("...ca,ad->...cd", mid_r, cos_a, precision=high) + jnp.einsum(
        "...ca,ad->...cd", mid_i, sin_a, precision=high
    )
    out_i = jnp.einsum("...ca,ad->...cd", mid_i, cos_a, precision=high) - jnp.einsum(
        "...ca,ad->...cd", mid_r, sin_a, precision=high
    )
    return (out_r, out_i)


def inverse_dft(spec_r, spec_i, tables):
    side_b, side_a, cos_b, sin_b, cos_a, sin_a, twist_r, twist_s = tables
    high = lax.Precision.HIGHEST
    back_r = jnp.einsum("...cd,da->...ca", spec_r, cos_a, precision=high) - jnp.einsum(
        "...cd,da->...ca", spec_i, sin_a, precision=high
    )
    back_i = jnp.einsum("...cd,da->...ca", spec_i, cos_a, precision=high) + jnp.einsum(
        "...cd,da->...ca", spec_r, sin_a, precision=high
    )
    turn_r = back_r * twist_r - back_i * twist_s
    turn_i = back_i * twist_r + back_r * twist_s
    whole = jnp.einsum("bc,...ca->...ba", cos_b, turn_r, precision=high) - jnp.einsum(
        "bc,...ca->...ba", sin_b, turn_i, precision=high
    )
    return whole / (side_b * side_a)


def convolve(fields, filt, tables):
    side_b, side_a = (tables[0], tables[1])
    length = side_b * side_a
    chans = fields.shape[1]
    stacked = jnp.concatenate([fields[0:1], filt[None], fields[1:]], axis=0).astype(jnp.float32)
    spec_r, spec_i = forward_dft(stacked.reshape(8, chans, side_b, side_a), tables)
    prod_r = spec_r[0] * spec_r[1] - spec_i[0] * spec_i[1]
    prod_i = spec_r[0] * spec_i[1] + spec_i[0] * spec_r[1]
    key_r, key_i = (spec_r[2:5], spec_i[2:5])
    val_r, val_i = (spec_r[5:8], spec_i[5:8])
    k_one_r, k_one_i = (jnp.roll(key_r, -1, axis=0), jnp.roll(key_i, -1, axis=0))
    k_two_r, k_two_i = (jnp.roll(key_r, -2, axis=0), jnp.roll(key_i, -2, axis=0))
    v_one_r, v_one_i = (jnp.roll(val_r, -1, axis=0), jnp.roll(val_i, -1, axis=0))
    v_two_r, v_two_i = (jnp.roll(val_r, -2, axis=0), jnp.roll(val_i, -2, axis=0))
    cross_r = k_one_r * v_two_r - k_one_i * v_two_i - (k_two_r * v_one_r - k_two_i * v_one_i)
    cross_i = k_one_r * v_two_i + k_one_i * v_two_r - (k_two_r * v_one_i + k_two_i * v_one_r)
    all_r = jnp.concatenate([prod_r[None], cross_r], axis=0)
    all_i = jnp.concatenate([prod_i[None], cross_i], axis=0)
    result = inverse_dft(all_r, all_i, tables).reshape(4, chans, length)
    inv_root = 1.0 / math.sqrt(length)
    scale = jnp.array([1.0, inv_root, inv_root, inv_root], dtype=jnp.float32)
    return (result * scale[:, None, None]).astype(jnp.bfloat16)


def plain_device(
    scalars,
    vectors,
    w_qkw_s,
    w_qkw_v,
    w_out_s,
    w_out_v,
    w_up,
    w_down,
    w_mix,
    w_gate,
    gains,
    pe_w1,
    pe_w2,
    pe_w3,
    rates,
):
    chans = scalars.shape[0]
    tok_local = scalars.shape[1]
    shards = lax.axis_size("seq")
    rank = lax.axis_index("seq")
    length = tok_local * shards
    depth = w_qkw_s.shape[0]
    tables = make_tables(length)
    local_pos = rank * tok_local + jnp.arange(tok_local, dtype=jnp.int32)
    made = jnp.stack(
        [
            filter_values(local_pos, length, pe_w1[layer], pe_w2[layer], pe_w3[layer], rates[layer])
            for layer in range(depth)
        ],
        axis=0,
    )
    filters = lax.all_to_all(made, "seq", split_axis=1, concat_axis=2, tiled=True)
    state_s = scalars.astype(jnp.float32)
    state_v = vectors.astype(jnp.float32)
    for layer in range(depth):
        normed_s = scalar_norm(state_s, gains[layer, 0]).astype(jnp.bfloat16)
        normed_v = vector_norm(state_v, gains[layer, 1]).astype(jnp.bfloat16)
        proj_s = jnp.dot(w_qkw_s[layer], normed_s, preferred_element_type=jnp.float32)
        query_s = proj_s[:chans].astype(jnp.bfloat16)
        signal_s = (proj_s[chans : 2 * chans] * proj_s[2 * chans :]).astype(jnp.bfloat16)
        proj_v = jnp.einsum(
            "oc,jct->jot", w_qkw_v[layer], normed_v, preferred_element_type=jnp.float32
        ).astype(jnp.bfloat16)
        query_v = proj_v[:, :chans]
        outgoing = jnp.concatenate(
            [signal_s[None], proj_v[:, chans : 2 * chans], proj_v[:, 2 * chans :]], axis=0
        )
        regrouped = lax.all_to_all(outgoing, "seq", split_axis=1, concat_axis=2, tiled=True)
        convolved = convolve(regrouped, filters[layer], tables)
        returned = lax.all_to_all(convolved, "seq", split_axis=2, concat_axis=1, tiled=True)
        conv_f = returned.astype(jnp.float32)
        qs_f = query_s.astype(jnp.float32)
        out_s = (
            qs_f * conv_f[0] + jnp.sum(query_v.astype(jnp.float32) * conv_f[1:], axis=0)
        ).astype(jnp.bfloat16)
        out_v = (qs_f[None] * conv_f[1:]).astype(jnp.bfloat16)
        state_s = state_s + jnp.dot(w_out_s[layer], out_s, preferred_element_type=jnp.float32)
        state_v = state_v + jnp.einsum(
            "oc,jct->jot", w_out_v[layer], out_v, preferred_element_type=jnp.float32
        )
        mlp_s = scalar_norm(state_s, gains[layer, 2]).astype(jnp.bfloat16)
        mlp_v = vector_norm(state_v, gains[layer, 3]).astype(jnp.bfloat16)
        hidden = jax.nn.gelu(
            jnp.dot(w_up[layer], mlp_s, preferred_element_type=jnp.float32)
        ).astype(jnp.bfloat16)
        gate = jax.nn.sigmoid(jnp.dot(w_gate[layer], mlp_s, preferred_element_type=jnp.float32))
        state_s = state_s + jnp.dot(w_down[layer], hidden, preferred_element_type=jnp.float32)
        state_v = (
            state_v
            + jnp.einsum("oc,jct->jot", w_mix[layer], mlp_v, preferred_element_type=jnp.float32)
            * gate[None]
        )
    return (state_s.astype(jnp.bfloat16), state_v.astype(jnp.bfloat16))


def reduced_sine(angle):
    turns = jnp.floor(angle * (1.0 / math.pi) + 0.5)
    rest = angle - turns * 3.140625
    rest = rest - turns * 9.67502593994140625e-4
    rest = rest - turns * 1.509957990978376432e-7
    half = turns * 0.5
    sign = 1.0 - 4.0 * (half - jnp.floor(half))
    sq = rest * rest
    poly = -2.5052108e-8
    poly = poly * sq + 2.7557319e-6
    poly = poly * sq - 1.9841270e-4
    poly = poly * sq + 8.3333333e-3
    poly = poly * sq - 1.6666667e-1
    return sign * (rest + rest * sq * poly)


def part_sum(one, two):
    if one is None:
        return two
    if two is None:
        return one
    return one + two


def part_diff(one, two):
    if two is None:
        return one
    if one is None:
        return -two
    return one - two


def turn(value, step, count):
    step = step % count
    real, imag = value
    if step == 0:
        return value
    if 4 * step == count:
        return (None if imag is None else -imag, real)
    if 4 * step == 3 * count:
        return (imag, None if real is None else -real)
    cos, sin = (math.cos(2 * math.pi * step / count), math.sin(2 * math.pi * step / count))
    if imag is None:
        return (real * cos, real * sin)
    if real is None:
        return (imag * -sin, imag * cos)
    return (real * cos - imag * sin, imag * cos + real * sin)


def real_fft(fields):
    count = len(fields)
    if count == 1:
        return [(fields[0], None)]
    if count == 2:
        return [(fields[0] + fields[1], None), (fields[0] - fields[1], None)]
    even, odd = (real_fft(fields[0::2]), real_fft(fields[1::2]))
    out = [None] * (count // 2 + 1)
    for k in range(count // 4 + 1):
        spun = turn(odd[k], -k, count)
        out[k] = (part_sum(even[k][0], spun[0]), part_sum(even[k][1], spun[1]))
        back = (part_diff(even[k][0], spun[0]), part_diff(spun[1], even[k][1]))
        if count // 2 - k != k:
            out[count // 2 - k] = back
    return out


def inverse_real_fft(spec, count):
    if count == 1:
        return [spec[0][0]]
    if count == 2:
        return [spec[0][0] + spec[1][0], spec[0][0] - spec[1][0]]
    even, odd = ([], [])
    for k in range(count // 4 + 1):
        one, two = (spec[k], spec[count // 2 - k])
        if 4 * k == count:
            even.append((one[0] * 2.0, None))
            odd.append((one[1] * -2.0, None))
            continue
        even.append((part_sum(one[0], two[0]), part_diff(one[1], two[1])))
        diff = (part_diff(one[0], two[0]), part_sum(one[1], two[1]))
        odd.append(turn(diff, k, count))
    out = [None] * count
    out[0::2] = inverse_real_fft(even, count // 2)
    out[1::2] = inverse_real_fft(odd, count // 2)
    return out


def local_tables(shards, tok_local):
    length = shards * tok_local
    freq = np.arange(shards // 2 + 1)[:, None, None] + shards * np.arange(tok_local)[None, None, :]
    angle = (np.arange(tok_local)[None, :, None] * freq % length) * (2.0 * np.pi / length)
    cos, sin = (np.cos(angle), np.sin(angle))
    fore = np.concatenate(
        [np.concatenate([cos, -sin], axis=2), np.concatenate([sin, cos], axis=2)], axis=1
    )
    return jnp.asarray(fore, jnp.float32)


def layers_kernel(shards, count, *refs):
    outside, refs = (refs[:count], refs[count:])
    scalars_out, vectors_out, *refs = refs
    inside, refs = (refs[:count], refs[count:])
    load_sem, state_s, state_v, query_s, query_v, *refs = refs
    fore, made_f, sent_x, got_x, sent_y, got_y, mid, inv, send_sem, recv_sem = refs
    scalars, vectors, w_qkw_s, w_qkw_v, w_out_s, w_out_v, w_up, w_down, w_mix, w_gate = inside[:10]
    gains, pe_w1, pe_w2, pe_w3, rates, fore_wide = inside[10:]
    loads = [
        pltpu.make_async_copy(outside[i], inside[i], load_sem.at[i]) for i in range(count)
    ]
    for i in (1, 3, 10, 0, 2, 11, 12, 13, 14, 15, 5, 8, 4, 6, 9, 7):
        loads[i].start()

    def need(*places):
        for i in places:
            loads[i].wait()

    grp = lax.axis_index("grp")
    me = lax.axis_index("seq")
    chans, tok = scalars.shape
    own = chans // shards
    length = shards * tok
    depth = w_qkw_s.shape[0]
    half = shards // 2 + 1
    f32, bf16 = (jnp.float32, jnp.bfloat16)
    mesh_id = pl.DeviceIdType.MESH

    barrier = pltpu.get_barrier_semaphore()

    def greet(step, carry):
        peer = lax.rem(me + step, shards)
        pl.semaphore_signal(barrier, inc=1, device_id=(grp, peer), device_id_type=mesh_id)
        return carry

    lax.fori_loop(1, shards, greet, 0)

    def copy_of(kind, src, dst, peer, lane):
        return pltpu.make_async_remote_copy(
            src_ref=src,
            dst_ref=dst,
            send_sem=send_sem.at[kind, peer],
            recv_sem=recv_sem.at[kind, lane],
            device_id=(grp, peer),
            device_id_type=mesh_id,
        )

    def send(kind, src, dst, rows):
        def body(turn, carry):
            side = lax.rem(turn, 2)
            step = shards // 2 + (1 - 2 * side) * ((turn + 1) // 2)
            peer = lax.rem(me + step, shards)
            copy_of(kind, src.at[peer, rows], dst.at[me, rows], peer, me).start()
            return carry

        lax.fori_loop(0, shards - 1, body, 0)
        dst[pl.ds(me, 1), rows] = src[pl.ds(me, 1), rows]

    def receive(kind, dst, rows):
        def body(step, carry):
            peer = lax.rem(me + step, shards)
            copy_of(kind, dst.at[peer, rows], dst.at[peer, rows], peer, peer).wait_recv()
            return carry

        lax.fori_loop(1, shards, body, 0)

    def sent(kind, src, rows):
        def body(step, carry):
            peer = lax.rem(me + step, shards)
            copy_of(kind, src.at[peer, rows], src.at[peer, rows], peer, peer).wait_send()
            return carry

        lax.fori_loop(1, shards, body, 0)

    def column(row):
        return jnp.broadcast_to(row, (tok, chans)).T

    def normed_scalar(field, gain):
        return (
            field * lax.rsqrt(jnp.mean(field * field, axis=0, keepdims=True) + 1e-05) * gain
        ).astype(bf16)

    def normed_vector(fields, gain):
        total = sum(jnp.sum(field * field, axis=0, keepdims=True) for field in fields)
        scale = lax.rsqrt(total * (1.0 / (3 * chans)) + 1e-05)
        return jnp.concatenate([(field * scale * gain).astype(bf16) for field in fields], axis=1)

    def make_filter(layer):
        freqs = pe_w1.shape[1] // 2
        high = lax.Precision.HIGHEST
        lhs_rows = (((0,), (0,)), ((), ()))
        pick = (
            lax.broadcasted_iota(jnp.int32, (own, chans), 1)
            == me * own + lax.broadcasted_iota(jnp.int32, (own, chans), 0)
        ).astype(f32)
        rate = jnp.sum(pick * rates[layer : layer + 1, :], axis=1, keepdims=True)
        third = lax.dot_general(
            pick, pe_w3[layer], (((1,), (1,)), ((), ())), precision=high, preferred_element_type=f32
        )
        span = tok * math.gcd(4, shards)
        for start in range(0, length, span):
            row = lax.broadcasted_iota(jnp.int32, (2 * freqs, span), 0)
            pos = start + lax.broadcasted_iota(jnp.int32, (2 * freqs, span), 1)
            is_cos = row < freqs
            turns = (jnp.where(is_cos, row + 1, row + 1 - freqs) * pos).astype(f32)
            turns = turns + jnp.where(is_cos, length / 4.0, 0.0)
            turns = turns - length * jnp.floor(turns * (1.0 / length))
            feats = reduced_sine(turns * (2.0 * math.pi / length))
            one = reduced_sine(
                lax.dot_general(
                    pe_w1[layer], feats, lhs_rows, precision=high, preferred_element_type=f32
                )
            )
            two = reduced_sine(
                jnp.dot(pe_w2[layer], one, precision=high, preferred_element_type=f32)
            )
            raw = jnp.dot(third, two, precision=high, preferred_element_type=f32)
            place = (start + lax.broadcasted_iota(jnp.int32, (own, span), 1)).astype(f32)
            made = raw * jnp.exp(-rate * place * (1.0 / length)) * (1.0 / math.sqrt(length))
            for r in range(span // tok):
                made_f[start // tok + r] = made[:, r * tok : (r + 1) * tok].astype(bf16)

    def spread(fields, row):
        spec = real_fft(fields)
        for k in range(half):
            real, imag = spec[k]
            mid[k, row : row + own, 0:tok] = real.astype(bf16)
            if imag is None:
                imag = jnp.zeros_like(real)
            mid[k, row : row + own, tok : 2 * tok] = imag.astype(bf16)

    def gather_back(layer, signal, scale):
        spec = []
        for k in range(half):
            imag = None if k in (0, half - 1) else inv[k, signal * own : (signal + 1) * own, tok : 2 * tok]
            spec.append((inv[k, signal * own : (signal + 1) * own, 0:tok], imag))
        out = inverse_real_fft(spec, shards)
        for r in range(shards):
            sent_y[layer, r, signal * own : (signal + 1) * own, :] = (out[r] * scale).astype(bf16)

    def incoming(ref, row):
        return [ref[r, row : row + own, :].astype(f32) for r in range(shards)]

    def times(one, two):
        return (one[0] * two[0] - one[1] * two[1], one[0] * two[1] + one[1] * two[0])

    def undo(spec, k):
        return lax.dot_general(
            spec, fore[k], (((1,), (1,)), ((), ())), preferred_element_type=f32
        )

    need(1)
    state_v[...] = vectors[...].astype(f32)
    vec_rows, sca_rows = (pl.ds(0, 6 * own), pl.ds(6 * own, own))
    for layer in range(depth):
        base = 4 * layer
        fields = [state_v[j] for j in range(3)]
        if layer == 0:
            need(10, 3)
        vn = normed_vector(fields, column(gains[layer, 1:2, :]))
        pv = jnp.dot(w_qkw_v[layer, chans:, :], vn, preferred_element_type=f32).astype(bf16)
        for j in range(3):
            cols = slice(j * tok, (j + 1) * tok)
            sent_x[layer, :, j * own : (j + 1) * own, :] = pv[:chans, cols].reshape(shards, own, tok)
            sent_x[layer, :, (3 + j) * own : (4 + j) * own, :] = pv[chans:, cols].reshape(
                shards, own, tok
            )
        if layer == 0:
            pl.semaphore_wait(barrier, shards - 1)
        send(base, sent_x.at[layer], got_x.at[layer], vec_rows)
        if layer == 0:
            need(0, 2)
            state_s[...] = scalars[...].astype(f32)
        sn = normed_scalar(state_s[...], column(gains[layer, 0:1, :]))
        ps = jnp.dot(w_qkw_s[layer, chans:, :], sn, preferred_element_type=f32)
        sent_x[layer, :, 6 * own : 7 * own, :] = (
            (ps[:chans] * ps[chans:]).astype(bf16).reshape(shards, own, tok)
        )
        send(base + 1, sent_x.at[layer], got_x.at[layer], sca_rows)
        query_s[...] = jnp.dot(w_qkw_s[layer, :chans, :], sn, preferred_element_type=f32).astype(bf16)
        query_v[...] = jnp.dot(w_qkw_v[layer, :chans, :], vn, preferred_element_type=f32).astype(bf16)
        if layer == 0:
            need(11, 12, 13, 14)
        make_filter(layer)
        spread(incoming(made_f, 0), 7 * own)
        if layer == 0:
            need(15)
            fore[...] = fore_wide[...].astype(bf16)

        receive(base, got_x.at[layer], vec_rows)
        for signal in range(6):
            spread(incoming(got_x.at[layer], signal * own), signal * own)
        for k in range(half):
            spec = jnp.dot(mid[k, : 6 * own, :], fore[k], preferred_element_type=f32)
            parts = [
                (spec[i * own : (i + 1) * own, :tok], spec[i * own : (i + 1) * own, tok:])
                for i in range(6)
            ]
            rows = []
            for j in range(3):
                plus = times(parts[(j + 1) % 3], parts[3 + (j + 2) % 3])
                minus = times(parts[(j + 2) % 3], parts[3 + (j + 1) % 3])
                rows.append(jnp.concatenate([plus[0] - minus[0], plus[1] - minus[1]], axis=1))
            inv[k, : 3 * own, :] = undo(jnp.concatenate(rows, axis=0).astype(bf16), k)
        for signal in range(3):
            gather_back(layer, signal, 1.0 / (length * math.sqrt(length)))
        send(base + 2, sent_y.at[layer], got_y.at[layer], pl.ds(0, 3 * own))

        receive(base + 1, got_x.at[layer], sca_rows)
        spread(incoming(got_x.at[layer], 6 * own), 6 * own)
        for k in range(half):
            spec = jnp.dot(mid[k, 6 * own :, :], fore[k], preferred_element_type=f32)
            prod = times((spec[:own, :tok], spec[:own, tok:]), (spec[own:, :tok], spec[own:, tok:]))
            inv[k, 3 * own :, :] = undo(jnp.concatenate(prod, axis=1).astype(bf16), k)
        gather_back(layer, 3, 1.0 / length)
        send(base + 3, sent_y.at[layer], got_y.at[layer], pl.ds(3 * own, own))

        if layer == 0:
            need(5, 8, 4, 6, 9, 7)
        receive(base + 2, got_y.at[layer], pl.ds(0, 3 * own))
        qs = query_s[...].astype(f32)
        out_v = []
        mixed = None
        for j in range(3):
            field = got_y[layer, :, j * own : (j + 1) * own, :].reshape(chans, tok).astype(f32)
            term = query_v[:, j * tok : (j + 1) * tok].astype(f32) * field
            mixed = term if mixed is None else mixed + term
            out_v.append((qs * field).astype(bf16))
        moved = jnp.dot(w_out_v[layer], jnp.concatenate(out_v, axis=1), preferred_element_type=f32)
        fields = [state_v[j] + moved[:, j * tok : (j + 1) * tok] for j in range(3)]
        vm = normed_vector(fields, column(gains[layer, 3:4, :]))
        mix = jnp.dot(w_mix[layer], vm, preferred_element_type=f32)
        receive(base + 3, got_y.at[layer], pl.ds(3 * own, own))
        field = got_y[layer, :, 3 * own : 4 * own, :].reshape(chans, tok).astype(f32)
        out_s = (qs * field + mixed).astype(bf16)
        now_s = state_s[...] + jnp.dot(w_out_s[layer], out_s, preferred_element_type=f32)
        sm = normed_scalar(now_s, column(gains[layer, 2:3, :]))
        hidden = jax.nn.gelu(jnp.dot(w_up[layer], sm, preferred_element_type=f32)).astype(bf16)
        gate = jax.nn.sigmoid(jnp.dot(w_gate[layer], sm, preferred_element_type=f32))
        now_s = now_s + jnp.dot(w_down[layer], hidden, preferred_element_type=f32)
        now_v = [fields[j] + mix[:, j * tok : (j + 1) * tok] * gate for j in range(3)]
        if layer + 1 < depth:
            state_s[...] = now_s
            for j in range(3):
                state_v[j] = now_v[j]
        else:
            scalars_out[...] = now_s.astype(bf16)
            for j in range(3):
                vectors_out[j] = now_v[j].astype(bf16)
    for layer in range(depth):
        base = 4 * layer
        sent(base, sent_x.at[layer], vec_rows)
        sent(base + 1, sent_x.at[layer], sca_rows)
        sent(base + 2, sent_y.at[layer], pl.ds(0, 3 * own))
        sent(base + 3, sent_y.at[layer], pl.ds(3 * own, own))


def per_device(*arrays):
    scalars, vectors, w_qkw_s = arrays[:3]
    chans, tok = scalars.shape
    shards = lax.axis_size("seq")
    depth = w_qkw_s.shape[0]
    own = chans // shards
    if tok % 128 or own % 16 or chans % shards or shards & (shards - 1) or shards < 4:
        return plain_device(*arrays)
    half = shards // 2 + 1
    f32, bf16 = (jnp.float32, jnp.bfloat16)
    arrays = list(arrays)
    arrays[11] = jnp.swapaxes(arrays[11], 1, 2)
    arrays[13] = jnp.swapaxes(arrays[13], 1, 2)
    arrays.append(local_tables(shards, tok))
    count = len(arrays)
    whole = pl.BlockSpec(memory_space=pltpu.VMEM)
    return pl.pallas_call(
        functools.partial(layers_kernel, shards, count),
        out_shape=(
            jax.ShapeDtypeStruct(scalars.shape, bf16),
            jax.ShapeDtypeStruct(vectors.shape, bf16),
        ),
        in_specs=[pl.BlockSpec(memory_space=pltpu.HBM)] * count,
        out_specs=(whole, whole),
        scratch_shapes=[pltpu.VMEM(array.shape, array.dtype) for array in arrays]
        + [
            pltpu.SemaphoreType.DMA((count,)),
            pltpu.VMEM((chans, tok), f32),
            pltpu.VMEM((3, chans, tok), f32),
            pltpu.VMEM((chans, tok), bf16),
            pltpu.VMEM((chans, 3 * tok), bf16),
            pltpu.VMEM((half, 2 * tok, 2 * tok), bf16),
            pltpu.VMEM((shards, own, tok), bf16),
            pltpu.VMEM((depth, shards, 7 * own, tok), bf16),
            pltpu.VMEM((depth, shards, 7 * own, tok), bf16),
            pltpu.VMEM((depth, shards, 4 * own, tok), bf16),
            pltpu.VMEM((depth, shards, 4 * own, tok), bf16),
            pltpu.VMEM((half, 8 * own, 2 * tok), bf16),
            pltpu.VMEM((half, 4 * own, 2 * tok), f32),
            pltpu.SemaphoreType.DMA((4 * depth, shards)),
            pltpu.SemaphoreType.DMA((4 * depth, shards)),
        ],
        compiler_params=pltpu.CompilerParams(
            collective_id=0, has_side_effects=True, vmem_limit_bytes=63 * 1024 * 1024
        ),
        name="hyena_layers",
    )(*arrays)


def solution(mesh):
    in_specs = (
        P(None, ("grp", "seq")),
        P(None, None, ("grp", "seq")),
        P(),
        P(),
        P(),
        P(),
        P(),
        P(),
        P(),
        P(),
        P(),
        P(),
        P(),
        P(),
        P(),
    )
    out_specs = (P(None, ("grp", "seq")), P(None, None, ("grp", "seq")))
    return jax.shard_map(
        per_device, mesh=mesh, in_specs=in_specs, out_specs=out_specs, check_vma=False
    )
```

```python
import functools
import math

import jax
import jax.numpy as jnp
import numpy as np
from jax import lax
from jax.experimental import pallas as pl
from jax.experimental.pallas import tpu as pltpu
from jax.sharding import PartitionSpec as P


def filter_values(positions, length, first, second, third, decay):
    count = first.shape[1] // 2
    freqs = jnp.arange(1, count + 1, dtype=jnp.int32)
    turns = freqs[:, None] * positions[None, :] % length
    angle = turns.astype(jnp.float32) * (2.0 * math.pi / length)
    feats = jnp.concatenate([jnp.cos(angle), jnp.sin(angle)], axis=0)
    hid_one = jnp.sin(jnp.dot(first, feats, precision=lax.Precision.HIGHEST))
    hid_two = jnp.sin(jnp.dot(second, hid_one, precision=lax.Precision.HIGHEST))
    raw = jnp.dot(third, hid_two, precision=lax.Precision.HIGHEST)
    envelope = jnp.exp(-decay[:, None] * positions[None, :].astype(jnp.float32) / length)
    return (raw * envelope / math.sqrt(length)).astype(jnp.bfloat16)


def scalar_norm(field, gain):
    return field * lax.rsqrt(jnp.mean(field * field, axis=0, keepdims=True) + 1e-05) * gain[:, None]


def vector_norm(field, gain):
    return (
        field
        * lax.rsqrt(jnp.mean(field * field, axis=(0, 1), keepdims=True) + 1e-05)
        * gain[None, :, None]
    )


def square_table(count):
    index = jnp.arange(count, dtype=jnp.int32)
    turns = index[:, None] * index[None, :] % count
    angle = turns.astype(jnp.float32) * (2.0 * math.pi / count)
    return (jnp.cos(angle), jnp.sin(angle))


def make_tables(length):
    side_b = 1
    for candidate in range(1, math.isqrt(length) + 1):
        if length % candidate == 0:
            side_b = candidate
    side_a = length // side_b
    cos_b, sin_b = square_table(side_b)
    cos_a, sin_a = square_table(side_a)
    rows_b = jnp.arange(side_b, dtype=jnp.int32)
    cols_a = jnp.arange(side_a, dtype=jnp.int32)
    angle = (rows_b[:, None] * cols_a[None, :]).astype(jnp.float32) * (2.0 * math.pi / length)
    return (side_b, side_a, cos_b, sin_b, cos_a, sin_a, jnp.cos(angle), jnp.sin(angle))


def forward_dft(signal, tables):
    side_b, side_a, cos_b, sin_b, cos_a, sin_a, twist_r, twist_s = tables
    high = lax.Precision.HIGHEST
    first_r = jnp.einsum("cb,...ba->...ca", cos_b, signal, precision=high)
    first_i = -jnp.einsum("cb,...ba->...ca", sin_b, signal, precision=high)
    mid_r = first_r * twist_r + first_i * twist_s
    mid_i = first_i * twist_r - first_r * twist_s
    out_r = jnp.einsum("...ca,ad->...cd", mid_r, cos_a, precision=high) + jnp.einsum(
        "...ca,ad->...cd", mid_i, sin_a, precision=high
    )
    out_i = jnp.einsum("...ca,ad->...cd", mid_i, cos_a, precision=high) - jnp.einsum(
        "...ca,ad->...cd", mid_r, sin_a, precision=high
    )
    return (out_r, out_i)


def inverse_dft(spec_r, spec_i, tables):
    side_b, side_a, cos_b, sin_b, cos_a, sin_a, twist_r, twist_s = tables
    high = lax.Precision.HIGHEST
    back_r = jnp.einsum("...cd,da->...ca", spec_r, cos_a, precision=high) - jnp.einsum(
        "...cd,da->...ca", spec_i, sin_a, precision=high
    )
    back_i = jnp.einsum("...cd,da->...ca", spec_i, cos_a, precision=high) + jnp.einsum(
        "...cd,da->...ca", spec_r, sin_a, precision=high
    )
    turn_r = back_r * twist_r - back_i * twist_s
    turn_i = back_i * twist_r + back_r * twist_s
    whole = jnp.einsum("bc,...ca->...ba", cos_b, turn_r, precision=high) - jnp.einsum(
        "bc,...ca->...ba", sin_b, turn_i, precision=high
    )
    return whole / (side_b * side_a)


def convolve(fields, filt, tables):
    side_b, side_a = (tables[0], tables[1])
    length = side_b * side_a
    chans = fields.shape[1]
    stacked = jnp.concatenate([fields[0:1], filt[None], fields[1:]], axis=0).astype(jnp.float32)
    spec_r, spec_i = forward_dft(stacked.reshape(8, chans, side_b, side_a), tables)
    prod_r = spec_r[0] * spec_r[1] - spec_i[0] * spec_i[1]
    prod_i = spec_r[0] * spec_i[1] + spec_i[0] * spec_r[1]
    key_r, key_i = (spec_r[2:5], spec_i[2:5])
    val_r, val_i = (spec_r[5:8], spec_i[5:8])
    k_one_r, k_one_i = (jnp.roll(key_r, -1, axis=0), jnp.roll(key_i, -1, axis=0))
    k_two_r, k_two_i = (jnp.roll(key_r, -2, axis=0), jnp.roll(key_i, -2, axis=0))
    v_one_r, v_one_i = (jnp.roll(val_r, -1, axis=0), jnp.roll(val_i, -1, axis=0))
    v_two_r, v_two_i = (jnp.roll(val_r, -2, axis=0), jnp.roll(val_i, -2, axis=0))
    cross_r = k_one_r * v_two_r - k_one_i * v_two_i - (k_two_r * v_one_r - k_two_i * v_one_i)
    cross_i = k_one_r * v_two_i + k_one_i * v_two_r - (k_two_r * v_one_i + k_two_i * v_one_r)
    all_r = jnp.concatenate([prod_r[None], cross_r], axis=0)
    all_i = jnp.concatenate([prod_i[None], cross_i], axis=0)
    result = inverse_dft(all_r, all_i, tables).reshape(4, chans, length)
    inv_root = 1.0 / math.sqrt(length)
    scale = jnp.array([1.0, inv_root, inv_root, inv_root], dtype=jnp.float32)
    return (result * scale[:, None, None]).astype(jnp.bfloat16)


def plain_device(
    scalars,
    vectors,
    w_qkw_s,
    w_qkw_v,
    w_out_s,
    w_out_v,
    w_up,
    w_down,
    w_mix,
    w_gate,
    gains,
    pe_w1,
    pe_w2,
    pe_w3,
    rates,
):
    chans = scalars.shape[0]
    tok_local = scalars.shape[1]
    shards = lax.axis_size("seq")
    rank = lax.axis_index("seq")
    length = tok_local * shards
    depth = w_qkw_s.shape[0]
    tables = make_tables(length)
    local_pos = rank * tok_local + jnp.arange(tok_local, dtype=jnp.int32)
    made = jnp.stack(
        [
            filter_values(local_pos, length, pe_w1[layer], pe_w2[layer], pe_w3[layer], rates[layer])
            for layer in range(depth)
        ],
        axis=0,
    )
    filters = lax.all_to_all(made, "seq", split_axis=1, concat_axis=2, tiled=True)
    state_s = scalars.astype(jnp.float32)
    state_v = vectors.astype(jnp.float32)
    for layer in range(depth):
        normed_s = scalar_norm(state_s, gains[layer, 0]).astype(jnp.bfloat16)
        normed_v = vector_norm(state_v, gains[layer, 1]).astype(jnp.bfloat16)
        proj_s = jnp.dot(w_qkw_s[layer], normed_s, preferred_element_type=jnp.float32)
        query_s = proj_s[:chans].astype(jnp.bfloat16)
        signal_s = (proj_s[chans : 2 * chans] * proj_s[2 * chans :]).astype(jnp.bfloat16)
        proj_v = jnp.einsum(
            "oc,jct->jot", w_qkw_v[layer], normed_v, preferred_element_type=jnp.float32
        ).astype(jnp.bfloat16)
        query_v = proj_v[:, :chans]
        outgoing = jnp.concatenate(
            [signal_s[None], proj_v[:, chans : 2 * chans], proj_v[:, 2 * chans :]], axis=0
        )
        regrouped = lax.all_to_all(outgoing, "seq", split_axis=1, concat_axis=2, tiled=True)
        convolved = convolve(regrouped, filters[layer], tables)
        returned = lax.all_to_all(convolved, "seq", split_axis=2, concat_axis=1, tiled=True)
        conv_f = returned.astype(jnp.float32)
        qs_f = query_s.astype(jnp.float32)
        out_s = (
            qs_f * conv_f[0] + jnp.sum(query_v.astype(jnp.float32) * conv_f[1:], axis=0)
        ).astype(jnp.bfloat16)
        out_v = (qs_f[None] * conv_f[1:]).astype(jnp.bfloat16)
        state_s = state_s + jnp.dot(w_out_s[layer], out_s, preferred_element_type=jnp.float32)
        state_v = state_v + jnp.einsum(
            "oc,jct->jot", w_out_v[layer], out_v, preferred_element_type=jnp.float32
        )
        mlp_s = scalar_norm(state_s, gains[layer, 2]).astype(jnp.bfloat16)
        mlp_v = vector_norm(state_v, gains[layer, 3]).astype(jnp.bfloat16)
        hidden = jax.nn.gelu(
            jnp.dot(w_up[layer], mlp_s, preferred_element_type=jnp.float32)
        ).astype(jnp.bfloat16)
        gate = jax.nn.sigmoid(jnp.dot(w_gate[layer], mlp_s, preferred_element_type=jnp.float32))
        state_s = state_s + jnp.dot(w_down[layer], hidden, preferred_element_type=jnp.float32)
        state_v = (
            state_v
            + jnp.einsum("oc,jct->jot", w_mix[layer], mlp_v, preferred_element_type=jnp.float32)
            * gate[None]
        )
    return (state_s.astype(jnp.bfloat16), state_v.astype(jnp.bfloat16))


def reduced_sine(angle):
    turns = jnp.floor(angle * (1.0 / math.pi) + 0.5)
    rest = angle - turns * 3.140625
    rest = rest - turns * 9.67502593994140625e-4
    rest = rest - turns * 1.509957990978376432e-7
    half = turns * 0.5
    sign = 1.0 - 4.0 * (half - jnp.floor(half))
    sq = rest * rest
    poly = -2.5052108e-8
    poly = poly * sq + 2.7557319e-6
    poly = poly * sq - 1.9841270e-4
    poly = poly * sq + 8.3333333e-3
    poly = poly * sq - 1.6666667e-1
    return sign * (rest + rest * sq * poly)


def part_sum(one, two):
    if one is None:
        return two
    if two is None:
        return one
    return one + two


def part_diff(one, two):
    if two is None:
        return one
    if one is None:
        return -two
    return one - two


def turn(value, step, count):
    step = step % count
    real, imag = value
    if step == 0:
        return value
    if 4 * step == count:
        return (None if imag is None else -imag, real)
    if 4 * step == 3 * count:
        return (imag, None if real is None else -real)
    cos, sin = (math.cos(2 * math.pi * step / count), math.sin(2 * math.pi * step / count))
    if imag is None:
        return (real * cos, real * sin)
    if real is None:
        return (imag * -sin, imag * cos)
    return (real * cos - imag * sin, imag * cos + real * sin)


def real_fft(fields):
    count = len(fields)
    if count == 1:
        return [(fields[0], None)]
    if count == 2:
        return [(fields[0] + fields[1], None), (fields[0] - fields[1], None)]
    even, odd = (real_fft(fields[0::2]), real_fft(fields[1::2]))
    out = [None] * (count // 2 + 1)
    for k in range(count // 4 + 1):
        spun = turn(odd[k], -k, count)
        out[k] = (part_sum(even[k][0], spun[0]), part_sum(even[k][1], spun[1]))
        back = (part_diff(even[k][0], spun[0]), part_diff(spun[1], even[k][1]))
        if count // 2 - k != k:
            out[count // 2 - k] = back
    return out


def inverse_real_fft(spec, count):
    if count == 1:
        return [spec[0][0]]
    if count == 2:
        return [spec[0][0] + spec[1][0], spec[0][0] - spec[1][0]]
    even, odd = ([], [])
    for k in range(count // 4 + 1):
        one, two = (spec[k], spec[count // 2 - k])
        if 4 * k == count:
            even.append((one[0] * 2.0, None))
            odd.append((one[1] * -2.0, None))
            continue
        even.append((part_sum(one[0], two[0]), part_diff(one[1], two[1])))
        diff = (part_diff(one[0], two[0]), part_sum(one[1], two[1]))
        odd.append(turn(diff, k, count))
    out = [None] * count
    out[0::2] = inverse_real_fft(even, count // 2)
    out[1::2] = inverse_real_fft(odd, count // 2)
    return out


def local_tables(shards, tok_local):
    length = shards * tok_local
    freq = np.arange(shards // 2 + 1)[:, None, None] + shards * np.arange(tok_local)[None, None, :]
    angle = (np.arange(tok_local)[None, :, None] * freq % length) * (2.0 * np.pi / length)
    cos, sin = (np.cos(angle), np.sin(angle))
    fore = np.concatenate(
        [np.concatenate([cos, -sin], axis=2), np.concatenate([sin, cos], axis=2)], axis=1
    )
    return jnp.asarray(fore, jnp.float32)


def layers_kernel(shards, count, *refs):
    outside, refs = (refs[:count], refs[count:])
    scalars_out, vectors_out, *refs = refs
    inside, refs = (refs[:count], refs[count:])
    load_sem, state_s, state_v, query_s, query_v, *refs = refs
    fore, made_f, sent_x, got_x, sent_y, got_y, mid, spec, inv, send_sem, recv_sem = refs
    scalars, vectors, w_qkw_s, w_qkw_v, w_out_s, w_out_v, w_up, w_down, w_mix, w_gate = inside[:10]
    gains, pe_w1, pe_w2, pe_w3, rates, fore_wide = inside[10:]
    loads = [
        pltpu.make_async_copy(outside[i], inside[i], load_sem.at[i]) for i in range(count)
    ]
    for i in (1, 3, 10, 0, 2, 11, 12, 13, 14, 15, 5, 8, 4, 6, 9, 7):
        loads[i].start()

    def need(*places):
        for i in places:
            loads[i].wait()

    grp = lax.axis_index("grp")
    me = lax.axis_index("seq")
    chans, tok = scalars.shape
    own = chans // shards
    length = shards * tok
    depth = w_qkw_s.shape[0]
    half = shards // 2 + 1
    f32, bf16 = (jnp.float32, jnp.bfloat16)
    mesh_id = pl.DeviceIdType.MESH

    barrier = pltpu.get_barrier_semaphore()

    def greet(step, carry):
        peer = lax.rem(me + step, shards)
        pl.semaphore_signal(barrier, inc=1, device_id=(grp, peer), device_id_type=mesh_id)
        return carry

    lax.fori_loop(1, shards, greet, 0)

    def copy_of(kind, src, dst, peer):
        return pltpu.make_async_remote_copy(
            src_ref=src,
            dst_ref=dst,
            send_sem=send_sem.at[kind],
            recv_sem=recv_sem.at[kind],
            device_id=(grp, peer),
            device_id_type=mesh_id,
        )

    def send(kind, src, dst, rows):
        def body(turn, carry):
            side = lax.rem(turn, 2)
            step = shards // 2 + (1 - 2 * side) * ((turn + 1) // 2)
            peer = lax.rem(me + step, shards)
            copy_of(kind, src.at[peer, rows], dst.at[me, rows], peer).start()
            return carry

        lax.fori_loop(0, shards - 1, body, 0)
        dst[pl.ds(me, 1), rows] = src[pl.ds(me, 1), rows]

    def all_of(kind, ref, rows):
        blocks = ref.at[pl.ds(0, shards - 1), rows]
        return copy_of(kind, blocks, blocks, lax.rem(me + 1, shards))

    def receive(kind, dst, rows):
        all_of(kind, dst, rows).wait_recv()

    def sent(kind, src, rows):
        all_of(kind, src, rows).wait_send()

    def column(row):
        return jnp.broadcast_to(row, (tok, chans)).T

    def normed_scalar(field, gain):
        return (
            field * lax.rsqrt(jnp.mean(field * field, axis=0, keepdims=True) + 1e-05) * gain
        ).astype(bf16)

    def normed_vector(fields, gain):
        total = sum(jnp.sum(field * field, axis=0, keepdims=True) for field in fields)
        scale = lax.rsqrt(total * (1.0 / (3 * chans)) + 1e-05)
        return jnp.concatenate([(field * scale * gain).astype(bf16) for field in fields], axis=1)

    def make_filter(layer):
        freqs = pe_w1.shape[1] // 2
        high = lax.Precision.HIGHEST
        lhs_rows = (((0,), (0,)), ((), ()))
        pick = (
            lax.broadcasted_iota(jnp.int32, (own, chans), 1)
            == me * own + lax.broadcasted_iota(jnp.int32, (own, chans), 0)
        ).astype(f32)
        rate = jnp.sum(pick * rates[layer : layer + 1, :], axis=1, keepdims=True)
        third = lax.dot_general(
            pick, pe_w3[layer], (((1,), (1,)), ((), ())), precision=high, preferred_element_type=f32
        )
        span = tok * math.gcd(4, shards)
        for start in range(0, length, span):
            row = lax.broadcasted_iota(jnp.int32, (2 * freqs, span), 0)
            pos = start + lax.broadcasted_iota(jnp.int32, (2 * freqs, span), 1)
            is_cos = row < freqs
            turns = (jnp.where(is_cos, row + 1, row + 1 - freqs) * pos).astype(f32)
            turns = turns + jnp.where(is_cos, length / 4.0, 0.0)
            turns = turns - length * jnp.floor(turns * (1.0 / length))
            feats = reduced_sine(turns * (2.0 * math.pi / length))
            one = reduced_sine(
                lax.dot_general(
                    pe_w1[layer], feats, lhs_rows, precision=high, preferred_element_type=f32
                )
            )
            two = reduced_sine(
                jnp.dot(pe_w2[layer], one, precision=high, preferred_element_type=f32)
            )
            raw = jnp.dot(third, two, precision=high, preferred_element_type=f32)
            place = (start + lax.broadcasted_iota(jnp.int32, (own, span), 1)).astype(f32)
            made = raw * jnp.exp(-rate * place * (1.0 / length)) * (1.0 / math.sqrt(length))
            for r in range(span // tok):
                made_f[start // tok + r] = made[:, r * tok : (r + 1) * tok].astype(bf16)

    def spread(fields, row):
        spec = real_fft(fields)
        for k in range(half):
            real, imag = spec[k]
            mid[k, row : row + own, 0:tok] = real.astype(bf16)
            if imag is None:
                imag = jnp.zeros_like(real)
            mid[k, row : row + own, tok : 2 * tok] = imag.astype(bf16)

    def gather_back(layer, signal, scale):
        spec = []
        for k in range(half):
            imag = None if k in (0, half - 1) else inv[k, signal * own : (signal + 1) * own, tok : 2 * tok]
            spec.append((inv[k, signal * own : (signal + 1) * own, 0:tok], imag))
        out = inverse_real_fft(spec, shards)
        for r in range(shards):
            sent_y[layer, r, signal * own : (signal + 1) * own, :] = (out[r] * scale).astype(bf16)

    def incoming(ref, row):
        return [ref[r, row : row + own, :].astype(f32) for r in range(shards)]

    def times(one, two):
        return (one[0] * two[0] - one[1] * two[1], one[0] * two[1] + one[1] * two[0])

    def undo(spec, k):
        return lax.dot_general(
            spec, fore[k], (((1,), (1,)), ((), ())), preferred_element_type=f32
        )

    need(1)
    state_v[...] = vectors[...].astype(f32)
    x_rows = (pl.ds(0, 4 * own), pl.ds(4 * own, 2 * own), pl.ds(6 * own, own))
    y_rows = (pl.ds(0, own), pl.ds(own, 2 * own), pl.ds(3 * own, own))
    key_slot, val_slot = ((4, 0, 1), (5, 2, 3))

    def part(k, slot):
        return (
            spec[k, slot * own : (slot + 1) * own, :tok],
            spec[k, slot * own : (slot + 1) * own, tok:],
        )

    def cross(k, j):
        one, two = ((j + 1) % 3, (j + 2) % 3)
        plus = times(part(k, key_slot[one]), part(k, val_slot[two]))
        minus = times(part(k, key_slot[two]), part(k, val_slot[one]))
        return jnp.concatenate([plus[0] - minus[0], plus[1] - minus[1]], axis=1)

    def transform(first, last):
        for k in range(half):
            spec[k, first * own : last * own, :] = jnp.dot(
                mid[k, first * own : last * own, :], fore[k], preferred_element_type=f32
            )

    for layer in range(depth):
        base = 6 * layer
        fields = [state_v[j] for j in range(3)]
        if layer == 0:
            need(10, 3)
        vn = normed_vector(fields, column(gains[layer, 1:2, :]))
        w_kw = w_qkw_v[layer, chans:, :]
        pv = jnp.dot(w_kw, vn[:, tok:], preferred_element_type=f32).astype(bf16)
        for slot in range(4):
            rows = slice((slot // 2) * chans, (slot // 2 + 1) * chans)
            cols = slice((slot % 2) * tok, (slot % 2 + 1) * tok)
            sent_x[layer, :, slot * own : (slot + 1) * own, :] = pv[rows, cols].reshape(
                shards, own, tok
            )
        if layer == 0:
            pl.semaphore_wait(barrier, shards - 1)
        send(base, sent_x.at[layer], got_x.at[layer], x_rows[0])
        pv = jnp.dot(w_kw, vn[:, :tok], preferred_element_type=f32).astype(bf16)
        for slot in range(2):
            rows = slice(slot * chans, (slot + 1) * chans)
            sent_x[layer, :, (4 + slot) * own : (5 + slot) * own, :] = pv[rows].reshape(
                shards, own, tok
            )
        send(base + 1, sent_x.at[layer], got_x.at[layer], x_rows[1])
        if layer == 0:
            need(0, 2)
            state_s[...] = scalars[...].astype(f32)
        sn = normed_scalar(state_s[...], column(gains[layer, 0:1, :]))
        ps = jnp.dot(w_qkw_s[layer, chans:, :], sn, preferred_element_type=f32)
        sent_x[layer, :, 6 * own : 7 * own, :] = (
            (ps[:chans] * ps[chans:]).astype(bf16).reshape(shards, own, tok)
        )
        send(base + 2, sent_x.at[layer], got_x.at[layer], x_rows[2])
        query_s[...] = jnp.dot(w_qkw_s[layer, :chans, :], sn, preferred_element_type=f32).astype(bf16)
        query_v[...] = jnp.dot(w_qkw_v[layer, :chans, :], vn, preferred_element_type=f32).astype(bf16)
        if layer == 0:
            need(11, 12, 13, 14)
        make_filter(layer)
        spread(incoming(made_f, 0), 7 * own)
        if layer == 0:
            need(15)
            fore[...] = fore_wide[...].astype(bf16)

        receive(base, got_x.at[layer], x_rows[0])
        for slot in range(4):
            spread(incoming(got_x.at[layer], slot * own), slot * own)
        transform(0, 4)
        for k in range(half):
            inv[k, :own, :] = undo(cross(k, 0).astype(bf16), k)
        gather_back(layer, 0, 1.0 / (length * math.sqrt(length)))
        send(base + 3, sent_y.at[layer], got_y.at[layer], y_rows[0])

        receive(base + 1, got_x.at[layer], x_rows[1])
        for slot in range(4, 6):
            spread(incoming(got_x.at[layer], slot * own), slot * own)
        transform(4, 6)
        for k in range(half):
            both = jnp.concatenate([cross(k, 1), cross(k, 2)], axis=0)
            inv[k, own : 3 * own, :] = undo(both.astype(bf16), k)
        for signal in range(1, 3):
            gather_back(layer, signal, 1.0 / (length * math.sqrt(length)))
        send(base + 4, sent_y.at[layer], got_y.at[layer], y_rows[1])

        receive(base + 2, got_x.at[layer], x_rows[2])
        spread(incoming(got_x.at[layer], 6 * own), 6 * own)
        transform(6, 8)
        for k in range(half):
            prod = times(part(k, 6), part(k, 7))
            inv[k, 3 * own :, :] = undo(jnp.concatenate(prod, axis=1).astype(bf16), k)
        gather_back(layer, 3, 1.0 / length)
        send(base + 5, sent_y.at[layer], got_y.at[layer], y_rows[2])

        if layer == 0:
            need(5, 8, 4, 6, 9, 7)
        qs = query_s[...].astype(f32)
        out_v = []
        mixed = None
        for j in range(3):
            if j < 2:
                receive(base + 3 + j, got_y.at[layer], y_rows[j])
            field = got_y[layer, :, j * own : (j + 1) * own, :].reshape(chans, tok).astype(f32)
            term = query_v[:, j * tok : (j + 1) * tok].astype(f32) * field
            mixed = term if mixed is None else mixed + term
            out_v.append((qs * field).astype(bf16))
        moved = jnp.dot(w_out_v[layer], jnp.concatenate(out_v, axis=1), preferred_element_type=f32)
        fields = [state_v[j] + moved[:, j * tok : (j + 1) * tok] for j in range(3)]
        vm = normed_vector(fields, column(gains[layer, 3:4, :]))
        mix = jnp.dot(w_mix[layer], vm, preferred_element_type=f32)
        receive(base + 5, got_y.at[layer], y_rows[2])
        field = got_y[layer, :, 3 * own : 4 * own, :].reshape(chans, tok).astype(f32)
        out_s = (qs * field + mixed).astype(bf16)
        now_s = state_s[...] + jnp.dot(w_out_s[layer], out_s, preferred_element_type=f32)
        sm = normed_scalar(now_s, column(gains[layer, 2:3, :]))
        hidden = jax.nn.gelu(jnp.dot(w_up[layer], sm, preferred_element_type=f32)).astype(bf16)
        gate = jax.nn.sigmoid(jnp.dot(w_gate[layer], sm, preferred_element_type=f32))
        now_s = now_s + jnp.dot(w_down[layer], hidden, preferred_element_type=f32)
        now_v = [fields[j] + mix[:, j * tok : (j + 1) * tok] * gate for j in range(3)]
        if layer + 1 < depth:
            state_s[...] = now_s
            for j in range(3):
                state_v[j] = now_v[j]
        else:
            scalars_out[...] = now_s.astype(bf16)
            for j in range(3):
                vectors_out[j] = now_v[j].astype(bf16)
    for layer in range(depth):
        for i in range(3):
            sent(6 * layer + i, sent_x.at[layer], x_rows[i])
            sent(6 * layer + 3 + i, sent_y.at[layer], y_rows[i])


def per_device(*arrays):
    scalars, vectors, w_qkw_s = arrays[:3]
    chans, tok = scalars.shape
    shards = lax.axis_size("seq")
    depth = w_qkw_s.shape[0]
    own = chans // shards
    if tok % 128 or own % 16 or chans % shards or shards & (shards - 1) or shards < 4:
        return plain_device(*arrays)
    half = shards // 2 + 1
    f32, bf16 = (jnp.float32, jnp.bfloat16)
    arrays = list(arrays)
    arrays[11] = jnp.swapaxes(arrays[11], 1, 2)
    arrays[13] = jnp.swapaxes(arrays[13], 1, 2)
    arrays.append(local_tables(shards, tok))
    count = len(arrays)
    whole = pl.BlockSpec(memory_space=pltpu.VMEM)
    return pl.pallas_call(
        functools.partial(layers_kernel, shards, count),
        out_shape=(
            jax.ShapeDtypeStruct(scalars.shape, bf16),
            jax.ShapeDtypeStruct(vectors.shape, bf16),
        ),
        in_specs=[pl.BlockSpec(memory_space=pltpu.HBM)] * count,
        out_specs=(whole, whole),
        scratch_shapes=[pltpu.VMEM(array.shape, array.dtype) for array in arrays]
        + [
            pltpu.SemaphoreType.DMA((count,)),
            pltpu.VMEM((chans, tok), f32),
            pltpu.VMEM((3, chans, tok), f32),
            pltpu.VMEM((chans, tok), bf16),
            pltpu.VMEM((chans, 3 * tok), bf16),
            pltpu.VMEM((half, 2 * tok, 2 * tok), bf16),
            pltpu.VMEM((shards, own, tok), bf16),
            pltpu.VMEM((depth, shards, 7 * own, tok), bf16),
            pltpu.VMEM((depth, shards, 7 * own, tok), bf16),
            pltpu.VMEM((depth, shards, 4 * own, tok), bf16),
            pltpu.VMEM((depth, shards, 4 * own, tok), bf16),
            pltpu.VMEM((half, 8 * own, 2 * tok), bf16),
            pltpu.VMEM((half, 8 * own, 2 * tok), f32),
            pltpu.VMEM((half, 4 * own, 2 * tok), f32),
            pltpu.SemaphoreType.DMA((6 * depth,)),
            pltpu.SemaphoreType.DMA((6 * depth,)),
        ],
        compiler_params=pltpu.CompilerParams(
            collective_id=0, has_side_effects=True, vmem_limit_bytes=63 * 1024 * 1024
        ),
        name="hyena_layers",
    )(*arrays)


def solution(mesh):
    in_specs = (
        P(None, ("grp", "seq")),
        P(None, None, ("grp", "seq")),
        P(),
        P(),
        P(),
        P(),
        P(),
        P(),
        P(),
        P(),
        P(),
        P(),
        P(),
        P(),
        P(),
    )
    out_specs = (P(None, ("grp", "seq")), P(None, None, ("grp", "seq")))
    return jax.shard_map(
        per_device, mesh=mesh, in_specs=in_specs, out_specs=out_specs, check_vma=False
    )
```

```python
import functools
import math

import jax
import jax.numpy as jnp
import numpy as np
from jax import lax
from jax.experimental import pallas as pl
from jax.experimental.pallas import tpu as pltpu
from jax.sharding import PartitionSpec as P


def filter_values(positions, length, first, second, third, decay):
    count = first.shape[1] // 2
    freqs = jnp.arange(1, count + 1, dtype=jnp.int32)
    turns = freqs[:, None] * positions[None, :] % length
    angle = turns.astype(jnp.float32) * (2.0 * math.pi / length)
    feats = jnp.concatenate([jnp.cos(angle), jnp.sin(angle)], axis=0)
    hid_one = jnp.sin(jnp.dot(first, feats, precision=lax.Precision.HIGHEST))
    hid_two = jnp.sin(jnp.dot(second, hid_one, precision=lax.Precision.HIGHEST))
    raw = jnp.dot(third, hid_two, precision=lax.Precision.HIGHEST)
    envelope = jnp.exp(-decay[:, None] * positions[None, :].astype(jnp.float32) / length)
    return (raw * envelope / math.sqrt(length)).astype(jnp.bfloat16)


def scalar_norm(field, gain):
    return field * lax.rsqrt(jnp.mean(field * field, axis=0, keepdims=True) + 1e-05) * gain[:, None]


def vector_norm(field, gain):
    return (
        field
        * lax.rsqrt(jnp.mean(field * field, axis=(0, 1), keepdims=True) + 1e-05)
        * gain[None, :, None]
    )


def square_table(count):
    index = jnp.arange(count, dtype=jnp.int32)
    turns = index[:, None] * index[None, :] % count
    angle = turns.astype(jnp.float32) * (2.0 * math.pi / count)
    return (jnp.cos(angle), jnp.sin(angle))


def make_tables(length):
    side_b = 1
    for candidate in range(1, math.isqrt(length) + 1):
        if length % candidate == 0:
            side_b = candidate
    side_a = length // side_b
    cos_b, sin_b = square_table(side_b)
    cos_a, sin_a = square_table(side_a)
    rows_b = jnp.arange(side_b, dtype=jnp.int32)
    cols_a = jnp.arange(side_a, dtype=jnp.int32)
    angle = (rows_b[:, None] * cols_a[None, :]).astype(jnp.float32) * (2.0 * math.pi / length)
    return (side_b, side_a, cos_b, sin_b, cos_a, sin_a, jnp.cos(angle), jnp.sin(angle))


def forward_dft(signal, tables):
    side_b, side_a, cos_b, sin_b, cos_a, sin_a, twist_r, twist_s = tables
    high = lax.Precision.HIGHEST
    first_r = jnp.einsum("cb,...ba->...ca", cos_b, signal, precision=high)
    first_i = -jnp.einsum("cb,...ba->...ca", sin_b, signal, precision=high)
    mid_r = first_r * twist_r + first_i * twist_s
    mid_i = first_i * twist_r - first_r * twist_s
    out_r = jnp.einsum("...ca,ad->...cd", mid_r, cos_a, precision=high) + jnp.einsum(
        "...ca,ad->...cd", mid_i, sin_a, precision=high
    )
    out_i = jnp.einsum("...ca,ad->...cd", mid_i, cos_a, precision=high) - jnp.einsum(
        "...ca,ad->...cd", mid_r, sin_a, precision=high
    )
    return (out_r, out_i)


def inverse_dft(spec_r, spec_i, tables):
    side_b, side_a, cos_b, sin_b, cos_a, sin_a, twist_r, twist_s = tables
    high = lax.Precision.HIGHEST
    back_r = jnp.einsum("...cd,da->...ca", spec_r, cos_a, precision=high) - jnp.einsum(
        "...cd,da->...ca", spec_i, sin_a, precision=high
    )
    back_i = jnp.einsum("...cd,da->...ca", spec_i, cos_a, precision=high) + jnp.einsum(
        "...cd,da->...ca", spec_r, sin_a, precision=high
    )
    turn_r = back_r * twist_r - back_i * twist_s
    turn_i = back_i * twist_r + back_r * twist_s
    whole = jnp.einsum("bc,...ca->...ba", cos_b, turn_r, precision=high) - jnp.einsum(
        "bc,...ca->...ba", sin_b, turn_i, precision=high
    )
    return whole / (side_b * side_a)


def convolve(fields, filt, tables):
    side_b, side_a = (tables[0], tables[1])
    length = side_b * side_a
    chans = fields.shape[1]
    stacked = jnp.concatenate([fields[0:1], filt[None], fields[1:]], axis=0).astype(jnp.float32)
    spec_r, spec_i = forward_dft(stacked.reshape(8, chans, side_b, side_a), tables)
    prod_r = spec_r[0] * spec_r[1] - spec_i[0] * spec_i[1]
    prod_i = spec_r[0] * spec_i[1] + spec_i[0] * spec_r[1]
    key_r, key_i = (spec_r[2:5], spec_i[2:5])
    val_r, val_i = (spec_r[5:8], spec_i[5:8])
    k_one_r, k_one_i = (jnp.roll(key_r, -1, axis=0), jnp.roll(key_i, -1, axis=0))
    k_two_r, k_two_i = (jnp.roll(key_r, -2, axis=0), jnp.roll(key_i, -2, axis=0))
    v_one_r, v_one_i = (jnp.roll(val_r, -1, axis=0), jnp.roll(val_i, -1, axis=0))
    v_two_r, v_two_i = (jnp.roll(val_r, -2, axis=0), jnp.roll(val_i, -2, axis=0))
    cross_r = k_one_r * v_two_r - k_one_i * v_two_i - (k_two_r * v_one_r - k_two_i * v_one_i)
    cross_i = k_one_r * v_two_i + k_one_i * v_two_r - (k_two_r * v_one_i + k_two_i * v_one_r)
    all_r = jnp.concatenate([prod_r[None], cross_r], axis=0)
    all_i = jnp.concatenate([prod_i[None], cross_i], axis=0)
    result = inverse_dft(all_r, all_i, tables).reshape(4, chans, length)
    inv_root = 1.0 / math.sqrt(length)
    scale = jnp.array([1.0, inv_root, inv_root, inv_root], dtype=jnp.float32)
    return (result * scale[:, None, None]).astype(jnp.bfloat16)


def plain_device(
    scalars,
    vectors,
    w_qkw_s,
    w_qkw_v,
    w_out_s,
    w_out_v,
    w_up,
    w_down,
    w_mix,
    w_gate,
    gains,
    pe_w1,
    pe_w2,
    pe_w3,
    rates,
):
    chans = scalars.shape[0]
    tok_local = scalars.shape[1]
    shards = lax.axis_size("seq")
    rank = lax.axis_index("seq")
    length = tok_local * shards
    depth = w_qkw_s.shape[0]
    tables = make_tables(length)
    local_pos = rank * tok_local + jnp.arange(tok_local, dtype=jnp.int32)
    made = jnp.stack(
        [
            filter_values(local_pos, length, pe_w1[layer], pe_w2[layer], pe_w3[layer], rates[layer])
            for layer in range(depth)
        ],
        axis=0,
    )
    filters = lax.all_to_all(made, "seq", split_axis=1, concat_axis=2, tiled=True)
    state_s = scalars.astype(jnp.float32)
    state_v = vectors.astype(jnp.float32)
    for layer in range(depth):
        normed_s = scalar_norm(state_s, gains[layer, 0]).astype(jnp.bfloat16)
        normed_v = vector_norm(state_v, gains[layer, 1]).astype(jnp.bfloat16)
        proj_s = jnp.dot(w_qkw_s[layer], normed_s, preferred_element_type=jnp.float32)
        query_s = proj_s[:chans].astype(jnp.bfloat16)
        signal_s = (proj_s[chans : 2 * chans] * proj_s[2 * chans :]).astype(jnp.bfloat16)
        proj_v = jnp.einsum(
            "oc,jct->jot", w_qkw_v[layer], normed_v, preferred_element_type=jnp.float32
        ).astype(jnp.bfloat16)
        query_v = proj_v[:, :chans]
        outgoing = jnp.concatenate(
            [signal_s[None], proj_v[:, chans : 2 * chans], proj_v[:, 2 * chans :]], axis=0
        )
        regrouped = lax.all_to_all(outgoing, "seq", split_axis=1, concat_axis=2, tiled=True)
        convolved = convolve(regrouped, filters[layer], tables)
        returned = lax.all_to_all(convolved, "seq", split_axis=2, concat_axis=1, tiled=True)
        conv_f = returned.astype(jnp.float32)
        qs_f = query_s.astype(jnp.float32)
        out_s = (
            qs_f * conv_f[0] + jnp.sum(query_v.astype(jnp.float32) * conv_f[1:], axis=0)
        ).astype(jnp.bfloat16)
        out_v = (qs_f[None] * conv_f[1:]).astype(jnp.bfloat16)
        state_s = state_s + jnp.dot(w_out_s[layer], out_s, preferred_element_type=jnp.float32)
        state_v = state_v + jnp.einsum(
            "oc,jct->jot", w_out_v[layer], out_v, preferred_element_type=jnp.float32
        )
        mlp_s = scalar_norm(state_s, gains[layer, 2]).astype(jnp.bfloat16)
        mlp_v = vector_norm(state_v, gains[layer, 3]).astype(jnp.bfloat16)
        hidden = jax.nn.gelu(
            jnp.dot(w_up[layer], mlp_s, preferred_element_type=jnp.float32)
        ).astype(jnp.bfloat16)
        gate = jax.nn.sigmoid(jnp.dot(w_gate[layer], mlp_s, preferred_element_type=jnp.float32))
        state_s = state_s + jnp.dot(w_down[layer], hidden, preferred_element_type=jnp.float32)
        state_v = (
            state_v
            + jnp.einsum("oc,jct->jot", w_mix[layer], mlp_v, preferred_element_type=jnp.float32)
            * gate[None]
        )
    return (state_s.astype(jnp.bfloat16), state_v.astype(jnp.bfloat16))


def reduced_sine(angle):
    turns = jnp.floor(angle * (1.0 / math.pi) + 0.5)
    rest = angle - turns * 3.140625
    rest = rest - turns * 9.67502593994140625e-4
    rest = rest - turns * 1.509957990978376432e-7
    half = turns * 0.5
    sign = 1.0 - 4.0 * (half - jnp.floor(half))
    sq = rest * rest
    poly = -2.5052108e-8
    poly = poly * sq + 2.7557319e-6
    poly = poly * sq - 1.9841270e-4
    poly = poly * sq + 8.3333333e-3
    poly = poly * sq - 1.6666667e-1
    return sign * (rest + rest * sq * poly)


def part_sum(one, two):
    if one is None:
        return two
    if two is None:
        return one
    return one + two


def part_diff(one, two):
    if two is None:
        return one
    if one is None:
        return -two
    return one - two


def turn(value, step, count):
    step = step % count
    real, imag = value
    if step == 0:
        return value
    if 4 * step == count:
        return (None if imag is None else -imag, real)
    if 4 * step == 3 * count:
        return (imag, None if real is None else -real)
    cos, sin = (math.cos(2 * math.pi * step / count), math.sin(2 * math.pi * step / count))
    if imag is None:
        return (real * cos, real * sin)
    if real is None:
        return (imag * -sin, imag * cos)
    return (real * cos - imag * sin, imag * cos + real * sin)


def real_fft(fields):
    count = len(fields)
    if count == 1:
        return [(fields[0], None)]
    if count == 2:
        return [(fields[0] + fields[1], None), (fields[0] - fields[1], None)]
    even, odd = (real_fft(fields[0::2]), real_fft(fields[1::2]))
    out = [None] * (count // 2 + 1)
    for k in range(count // 4 + 1):
        spun = turn(odd[k], -k, count)
        out[k] = (part_sum(even[k][0], spun[0]), part_sum(even[k][1], spun[1]))
        back = (part_diff(even[k][0], spun[0]), part_diff(spun[1], even[k][1]))
        if count // 2 - k != k:
            out[count // 2 - k] = back
    return out


def inverse_real_fft(spec, count):
    if count == 1:
        return [spec[0][0]]
    if count == 2:
        return [spec[0][0] + spec[1][0], spec[0][0] - spec[1][0]]
    even, odd = ([], [])
    for k in range(count // 4 + 1):
        one, two = (spec[k], spec[count // 2 - k])
        if 4 * k == count:
            even.append((one[0] * 2.0, None))
            odd.append((one[1] * -2.0, None))
            continue
        even.append((part_sum(one[0], two[0]), part_diff(one[1], two[1])))
        diff = (part_diff(one[0], two[0]), part_sum(one[1], two[1]))
        odd.append(turn(diff, k, count))
    out = [None] * count
    out[0::2] = inverse_real_fft(even, count // 2)
    out[1::2] = inverse_real_fft(odd, count // 2)
    return out


def local_tables(shards, tok_local):
    length = shards * tok_local
    freq = np.arange(shards // 2 + 1)[:, None, None] + shards * np.arange(tok_local)[None, None, :]
    angle = (np.arange(tok_local)[None, :, None] * freq % length) * (2.0 * np.pi / length)
    cos, sin = (np.cos(angle), np.sin(angle))
    fore = np.concatenate(
        [np.concatenate([cos, -sin], axis=2), np.concatenate([sin, cos], axis=2)], axis=1
    )
    return jnp.asarray(fore, jnp.float32)


def layers_kernel(shards, count, *refs):
    outside, refs = (refs[:count], refs[count:])
    scalars_out, vectors_out, *refs = refs
    inside, refs = (refs[:count], refs[count:])
    load_sem, state_s, state_v, columns, ready_s, query_s, query_v, *refs = refs
    fore, made_f, sent_x, got_x, sent_y, got_y, mid, spec, inv, send_sem, recv_sem = refs
    scalars, vectors, w_qkw_s, w_qkw_v, w_out_s, w_out_v, w_up, w_down, w_mix, w_gate = inside[:10]
    gains, pe_w1, pe_w2, pe_w3, rates, fore_wide = inside[10:]
    loads = [
        pltpu.make_async_copy(outside[i], inside[i], load_sem.at[i]) for i in range(count)
    ]
    for i in (1, 3, 10, 0, 2, 11, 12, 13, 14, 15, 5, 8, 4, 6, 9, 7):
        loads[i].start()

    def need(*places):
        for i in places:
            loads[i].wait()

    grp = lax.axis_index("grp")
    me = lax.axis_index("seq")
    chans, tok = scalars.shape
    own = chans // shards
    length = shards * tok
    depth = w_qkw_s.shape[0]
    half = shards // 2 + 1
    f32, bf16 = (jnp.float32, jnp.bfloat16)
    mesh_id = pl.DeviceIdType.MESH

    barrier = pltpu.get_barrier_semaphore()

    def greet(step, carry):
        peer = lax.rem(me + step, shards)
        pl.semaphore_signal(barrier, inc=1, device_id=(grp, peer), device_id_type=mesh_id)
        return carry

    lax.fori_loop(1, shards, greet, 0)

    def copy_of(kind, src, dst, peer):
        return pltpu.make_async_remote_copy(
            src_ref=src,
            dst_ref=dst,
            send_sem=send_sem.at[kind],
            recv_sem=recv_sem.at[kind],
            device_id=(grp, peer),
            device_id_type=mesh_id,
        )

    def send(kind, src, dst, rows):
        def body(turn, carry):
            side = lax.rem(turn, 2)
            step = shards // 2 + (1 - 2 * side) * ((turn + 1) // 2)
            peer = lax.rem(me + step, shards)
            copy_of(kind, src.at[peer, rows], dst.at[me, rows], peer).start()
            return carry

        lax.fori_loop(0, shards - 1, body, 0)
        dst[pl.ds(me, 1), rows] = src[pl.ds(me, 1), rows]

    def all_of(kind, ref, rows):
        blocks = ref.at[pl.ds(0, shards - 1), rows]
        return copy_of(kind, blocks, blocks, lax.rem(me + 1, shards))

    def receive(kind, dst, rows):
        all_of(kind, dst, rows).wait_recv()

    def sent(kind, src, rows):
        all_of(kind, src, rows).wait_send()

    def column(row):
        return jnp.broadcast_to(row, (tok, chans)).T

    def normed_scalar(field, gain):
        return (
            field * lax.rsqrt(jnp.mean(field * field, axis=0, keepdims=True) + 1e-05) * gain
        ).astype(bf16)

    def normed_vector(fields, gain):
        total = sum(jnp.sum(field * field, axis=0, keepdims=True) for field in fields)
        scale = lax.rsqrt(total * (1.0 / (3 * chans)) + 1e-05)
        return jnp.concatenate([(field * scale * gain).astype(bf16) for field in fields], axis=1)

    def make_filter(layer):
        freqs = pe_w1.shape[1] // 2
        high = lax.Precision.HIGHEST
        lhs_rows = (((0,), (0,)), ((), ()))
        pick = (
            lax.broadcasted_iota(jnp.int32, (own, chans), 1)
            == me * own + lax.broadcasted_iota(jnp.int32, (own, chans), 0)
        ).astype(f32)
        rate = jnp.sum(pick * rates[layer : layer + 1, :], axis=1, keepdims=True)
        third = lax.dot_general(
            pick, pe_w3[layer], (((1,), (1,)), ((), ())), precision=high, preferred_element_type=f32
        )
        span = tok * math.gcd(4, shards)
        for start in range(0, length, span):
            row = lax.broadcasted_iota(jnp.int32, (2 * freqs, span), 0)
            pos = start + lax.broadcasted_iota(jnp.int32, (2 * freqs, span), 1)
            is_cos = row < freqs
            turns = (jnp.where(is_cos, row + 1, row + 1 - freqs) * pos).astype(f32)
            turns = turns + jnp.where(is_cos, length / 4.0, 0.0)
            turns = turns - length * jnp.floor(turns * (1.0 / length))
            feats = reduced_sine(turns * (2.0 * math.pi / length))
            one = reduced_sine(
                lax.dot_general(
                    pe_w1[layer], feats, lhs_rows, precision=high, preferred_element_type=f32
                )
            )
            two = reduced_sine(
                jnp.dot(pe_w2[layer], one, precision=high, preferred_element_type=f32)
            )
            raw = jnp.dot(third, two, precision=high, preferred_element_type=f32)
            place = (start + lax.broadcasted_iota(jnp.int32, (own, span), 1)).astype(f32)
            made = raw * jnp.exp(-rate * place * (1.0 / length)) * (1.0 / math.sqrt(length))
            for r in range(span // tok):
                made_f[start // tok + r] = made[:, r * tok : (r + 1) * tok].astype(bf16)

    def spread(fields, row):
        spec = real_fft(fields)
        for k in range(half):
            real, imag = spec[k]
            mid[k, row : row + own, 0:tok] = real.astype(bf16)
            if imag is None:
                imag = jnp.zeros_like(real)
            mid[k, row : row + own, tok : 2 * tok] = imag.astype(bf16)

    def gather_back(layer, signal, scale):
        spec = []
        for k in range(half):
            imag = None if k in (0, half - 1) else inv[k, signal * own : (signal + 1) * own, tok : 2 * tok]
            spec.append((inv[k, signal * own : (signal + 1) * own, 0:tok], imag))
        out = inverse_real_fft(spec, shards)
        for r in range(shards):
            sent_y[layer, r, signal * own : (signal + 1) * own, :] = (out[r] * scale).astype(bf16)

    def incoming(ref, row):
        return [ref[r, row : row + own, :].astype(f32) for r in range(shards)]

    def times(one, two):
        return (one[0] * two[0] - one[1] * two[1], one[0] * two[1] + one[1] * two[0])

    def undo(spec, k):
        return lax.dot_general(
            spec, fore[k], (((1,), (1,)), ((), ())), preferred_element_type=f32
        )

    need(1)
    state_v[...] = vectors[...].astype(f32)
    x_rows = (pl.ds(0, 4 * own), pl.ds(4 * own, 2 * own), pl.ds(6 * own, own))
    y_rows = (pl.ds(0, own), pl.ds(own, 2 * own), pl.ds(3 * own, own))
    key_slot, val_slot = ((4, 0, 1), (5, 2, 3))

    def part(k, slot):
        return (
            spec[k, slot * own : (slot + 1) * own, :tok],
            spec[k, slot * own : (slot + 1) * own, tok:],
        )

    def cross(k, j):
        one, two = ((j + 1) % 3, (j + 2) % 3)
        plus = times(part(k, key_slot[one]), part(k, val_slot[two]))
        minus = times(part(k, key_slot[two]), part(k, val_slot[one]))
        return jnp.concatenate([plus[0] - minus[0], plus[1] - minus[1]], axis=1)

    def transform(first, last):
        for k in range(half):
            spec[k, first * own : last * own, :] = jnp.dot(
                mid[k, first * own : last * own, :], fore[k], preferred_element_type=f32
            )

    def finish_scalar(layer):
        wide = jnp.dot(w_up[layer], ready_s[...], preferred_element_type=f32)
        hidden = jax.nn.gelu(wide).astype(bf16)
        return state_s[...] + jnp.dot(w_down[layer], hidden, preferred_element_type=f32)

    for layer in range(depth):
        base = 6 * layer
        fields = [state_v[j] for j in range(3)]
        if layer == 0:
            need(10, 3)
            columns[1] = column(gains[0, 1:2, :])
        vn = normed_vector(fields, columns[4 * layer + 1])
        w_kw = w_qkw_v[layer, chans:, :]
        pv = jnp.dot(w_kw, vn[:, tok:], preferred_element_type=f32).astype(bf16)
        for slot in range(4):
            rows = slice((slot // 2) * chans, (slot // 2 + 1) * chans)
            cols = slice((slot % 2) * tok, (slot % 2 + 1) * tok)
            sent_x[layer, :, slot * own : (slot + 1) * own, :] = pv[rows, cols].reshape(
                shards, own, tok
            )
        if layer == 0:
            pl.semaphore_wait(barrier, shards - 1)
        send(base, sent_x.at[layer], got_x.at[layer], x_rows[0])
        pv = jnp.dot(w_kw, vn[:, :tok], preferred_element_type=f32).astype(bf16)
        for slot in range(2):
            rows = slice(slot * chans, (slot + 1) * chans)
            sent_x[layer, :, (4 + slot) * own : (5 + slot) * own, :] = pv[rows].reshape(
                shards, own, tok
            )
        send(base + 1, sent_x.at[layer], got_x.at[layer], x_rows[1])
        if layer == 0:
            need(0, 2)
            state_s[...] = scalars[...].astype(f32)
            columns[0] = column(gains[0, 0:1, :])
        else:
            state_s[...] = finish_scalar(layer - 1)
        sn = normed_scalar(state_s[...], columns[4 * layer])
        ps = jnp.dot(w_qkw_s[layer, chans:, :], sn, preferred_element_type=f32)
        sent_x[layer, :, 6 * own : 7 * own, :] = (
            (ps[:chans] * ps[chans:]).astype(bf16).reshape(shards, own, tok)
        )
        send(base + 2, sent_x.at[layer], got_x.at[layer], x_rows[2])
        query_s[...] = jnp.dot(w_qkw_s[layer, :chans, :], sn, preferred_element_type=f32).astype(bf16)
        query_v[...] = jnp.dot(w_qkw_v[layer, :chans, :], vn, preferred_element_type=f32).astype(bf16)
        if layer == 0:
            for place in range(2, 4 * depth):
                columns[place] = column(gains[place // 4, place % 4 : place % 4 + 1, :])
            need(11, 12, 13, 14)
        make_filter(layer)
        spread(incoming(made_f, 0), 7 * own)
        if layer == 0:
            need(15)
            fore[...] = fore_wide[...].astype(bf16)

        receive(base, got_x.at[layer], x_rows[0])
        for slot in range(4):
            spread(incoming(got_x.at[layer], slot * own), slot * own)
        transform(0, 4)
        for k in range(half):
            inv[k, :own, :] = undo(cross(k, 0).astype(bf16), k)
        gather_back(layer, 0, 1.0 / (length * math.sqrt(length)))
        send(base + 3, sent_y.at[layer], got_y.at[layer], y_rows[0])

        receive(base + 1, got_x.at[layer], x_rows[1])
        for slot in range(4, 6):
            spread(incoming(got_x.at[layer], slot * own), slot * own)
        transform(4, 6)
        for k in range(half):
            both = jnp.concatenate([cross(k, 1), cross(k, 2)], axis=0)
            inv[k, own : 3 * own, :] = undo(both.astype(bf16), k)
        for signal in range(1, 3):
            gather_back(layer, signal, 1.0 / (length * math.sqrt(length)))
        send(base + 4, sent_y.at[layer], got_y.at[layer], y_rows[1])

        receive(base + 2, got_x.at[layer], x_rows[2])
        spread(incoming(got_x.at[layer], 6 * own), 6 * own)
        transform(6, 8)
        for k in range(half):
            prod = times(part(k, 6), part(k, 7))
            inv[k, 3 * own :, :] = undo(jnp.concatenate(prod, axis=1).astype(bf16), k)
        gather_back(layer, 3, 1.0 / length)
        send(base + 5, sent_y.at[layer], got_y.at[layer], y_rows[2])

        if layer == 0:
            need(5, 8, 4, 6, 9, 7)
        qs = query_s[...].astype(f32)
        out_v = []
        mixed = None
        for j in range(3):
            if j < 2:
                receive(base + 3 + j, got_y.at[layer], y_rows[j])
            field = got_y[layer, :, j * own : (j + 1) * own, :].reshape(chans, tok).astype(f32)
            term = query_v[:, j * tok : (j + 1) * tok].astype(f32) * field
            mixed = term if mixed is None else mixed + term
            out_v.append((qs * field).astype(bf16))
        moved = jnp.dot(w_out_v[layer], jnp.concatenate(out_v, axis=1), preferred_element_type=f32)
        fields = [state_v[j] + moved[:, j * tok : (j + 1) * tok] for j in range(3)]
        vm = normed_vector(fields, columns[4 * layer + 3])
        mix = jnp.dot(w_mix[layer], vm, preferred_element_type=f32)
        receive(base + 5, got_y.at[layer], y_rows[2])
        field = got_y[layer, :, 3 * own : 4 * own, :].reshape(chans, tok).astype(f32)
        out_s = (qs * field + mixed).astype(bf16)
        now_s = state_s[...] + jnp.dot(w_out_s[layer], out_s, preferred_element_type=f32)
        sm = normed_scalar(now_s, columns[4 * layer + 2])
        gate = jax.nn.sigmoid(jnp.dot(w_gate[layer], sm, preferred_element_type=f32))
        now_v = [fields[j] + mix[:, j * tok : (j + 1) * tok] * gate for j in range(3)]
        ready_s[...] = sm
        state_s[...] = now_s
        if layer + 1 < depth:
            for j in range(3):
                state_v[j] = now_v[j]
        else:
            for j in range(3):
                vectors_out[j] = now_v[j].astype(bf16)
            scalars_out[...] = finish_scalar(layer).astype(bf16)
    for layer in range(depth):
        for i in range(3):
            sent(6 * layer + i, sent_x.at[layer], x_rows[i])
            sent(6 * layer + 3 + i, sent_y.at[layer], y_rows[i])


def place_results(scalars, vectors, scalars_out, vectors_out, sem):
    copies = [
        pltpu.make_async_copy(vectors, vectors_out, sem.at[0]),
        pltpu.make_async_copy(scalars, scalars_out, sem.at[1]),
    ]
    for copy in copies:
        copy.start()
    for copy in copies:
        copy.wait()


def per_device(*arrays):
    scalars, vectors, w_qkw_s = arrays[:3]
    chans, tok = scalars.shape
    shards = lax.axis_size("seq")
    depth = w_qkw_s.shape[0]
    own = chans // shards
    if tok % 128 or own % 16 or chans % shards or shards & (shards - 1) or shards < 4:
        return plain_device(*arrays)
    half = shards // 2 + 1
    f32, bf16 = (jnp.float32, jnp.bfloat16)
    arrays = list(arrays)
    arrays[11] = jnp.swapaxes(arrays[11], 1, 2)
    arrays[13] = jnp.swapaxes(arrays[13], 1, 2)
    arrays.append(local_tables(shards, tok))
    count = len(arrays)
    whole = pl.BlockSpec(memory_space=pltpu.VMEM)
    made = pl.pallas_call(
        functools.partial(layers_kernel, shards, count),
        out_shape=(
            jax.ShapeDtypeStruct(scalars.shape, bf16),
            jax.ShapeDtypeStruct(vectors.shape, bf16),
        ),
        in_specs=[pl.BlockSpec(memory_space=pltpu.HBM)] * count,
        out_specs=(whole, whole),
        scratch_shapes=[pltpu.VMEM(array.shape, array.dtype) for array in arrays]
        + [
            pltpu.SemaphoreType.DMA((count,)),
            pltpu.VMEM((chans, tok), f32),
            pltpu.VMEM((3, chans, tok), f32),
            pltpu.VMEM((4 * depth, chans, tok), f32),
            pltpu.VMEM((chans, tok), bf16),
            pltpu.VMEM((chans, tok), bf16),
            pltpu.VMEM((chans, 3 * tok), bf16),
            pltpu.VMEM((half, 2 * tok, 2 * tok), bf16),
            pltpu.VMEM((shards, own, tok), bf16),
            pltpu.VMEM((depth, shards, 7 * own, tok), bf16),
            pltpu.VMEM((depth, shards, 7 * own, tok), bf16),
            pltpu.VMEM((depth, shards, 4 * own, tok), bf16),
            pltpu.VMEM((depth, shards, 4 * own, tok), bf16),
            pltpu.VMEM((half, 8 * own, 2 * tok), bf16),
            pltpu.VMEM((half, 8 * own, 2 * tok), f32),
            pltpu.VMEM((half, 4 * own, 2 * tok), f32),
            pltpu.SemaphoreType.DMA((6 * depth,)),
            pltpu.SemaphoreType.DMA((6 * depth,)),
        ],
        compiler_params=pltpu.CompilerParams(
            collective_id=0, has_side_effects=True, vmem_limit_bytes=63 * 1024 * 1024
        ),
        name="hyena_layers",
    )(*arrays)
    held = pl.BlockSpec(memory_space=pltpu.HBM)
    return pl.pallas_call(
        place_results,
        out_shape=tuple(jax.ShapeDtypeStruct(one.shape, one.dtype) for one in made),
        in_specs=[held, held],
        out_specs=(held, held),
        scratch_shapes=[pltpu.SemaphoreType.DMA((2,))],
        compiler_params=pltpu.CompilerParams(vmem_limit_bytes=63 * 1024 * 1024),
        name="place_results",
    )(*made)


def solution(mesh):
    in_specs = (
        P(None, ("grp", "seq")),
        P(None, None, ("grp", "seq")),
        P(),
        P(),
        P(),
        P(),
        P(),
        P(),
        P(),
        P(),
        P(),
        P(),
        P(),
        P(),
        P(),
    )
    out_specs = (P(None, ("grp", "seq")), P(None, None, ("grp", "seq")))
    return jax.shard_map(
        per_device, mesh=mesh, in_specs=in_specs, out_specs=out_specs, check_vma=False
    )
```

```python
import functools
import math

import jax
import jax.numpy as jnp
import numpy as np
from jax import lax
from jax.experimental import pallas as pl
from jax.experimental.pallas import tpu as pltpu
from jax.sharding import PartitionSpec as P


def filter_values(positions, length, first, second, third, decay):
    count = first.shape[1] // 2
    freqs = jnp.arange(1, count + 1, dtype=jnp.int32)
    turns = freqs[:, None] * positions[None, :] % length
    angle = turns.astype(jnp.float32) * (2.0 * math.pi / length)
    feats = jnp.concatenate([jnp.cos(angle), jnp.sin(angle)], axis=0)
    hid_one = jnp.sin(jnp.dot(first, feats, precision=lax.Precision.HIGHEST))
    hid_two = jnp.sin(jnp.dot(second, hid_one, precision=lax.Precision.HIGHEST))
    raw = jnp.dot(third, hid_two, precision=lax.Precision.HIGHEST)
    envelope = jnp.exp(-decay[:, None] * positions[None, :].astype(jnp.float32) / length)
    return (raw * envelope / math.sqrt(length)).astype(jnp.bfloat16)


def scalar_norm(field, gain):
    return field * lax.rsqrt(jnp.mean(field * field, axis=0, keepdims=True) + 1e-05) * gain[:, None]


def vector_norm(field, gain):
    return (
        field
        * lax.rsqrt(jnp.mean(field * field, axis=(0, 1), keepdims=True) + 1e-05)
        * gain[None, :, None]
    )


def square_table(count):
    index = jnp.arange(count, dtype=jnp.int32)
    turns = index[:, None] * index[None, :] % count
    angle = turns.astype(jnp.float32) * (2.0 * math.pi / count)
    return (jnp.cos(angle), jnp.sin(angle))


def make_tables(length):
    side_b = 1
    for candidate in range(1, math.isqrt(length) + 1):
        if length % candidate == 0:
            side_b = candidate
    side_a = length // side_b
    cos_b, sin_b = square_table(side_b)
    cos_a, sin_a = square_table(side_a)
    rows_b = jnp.arange(side_b, dtype=jnp.int32)
    cols_a = jnp.arange(side_a, dtype=jnp.int32)
    angle = (rows_b[:, None] * cols_a[None, :]).astype(jnp.float32) * (2.0 * math.pi / length)
    return (side_b, side_a, cos_b, sin_b, cos_a, sin_a, jnp.cos(angle), jnp.sin(angle))


def forward_dft(signal, tables):
    side_b, side_a, cos_b, sin_b, cos_a, sin_a, twist_r, twist_s = tables
    high = lax.Precision.HIGHEST
    first_r = jnp.einsum("cb,...ba->...ca", cos_b, signal, precision=high)
    first_i = -jnp.einsum("cb,...ba->...ca", sin_b, signal, precision=high)
    mid_r = first_r * twist_r + first_i * twist_s
    mid_i = first_i * twist_r - first_r * twist_s
    out_r = jnp.einsum("...ca,ad->...cd", mid_r, cos_a, precision=high) + jnp.einsum(
        "...ca,ad->...cd", mid_i, sin_a, precision=high
    )
    out_i = jnp.einsum("...ca,ad->...cd", mid_i, cos_a, precision=high) - jnp.einsum(
        "...ca,ad->...cd", mid_r, sin_a, precision=high
    )
    return (out_r, out_i)


def inverse_dft(spec_r, spec_i, tables):
    side_b, side_a, cos_b, sin_b, cos_a, sin_a, twist_r, twist_s = tables
    high = lax.Precision.HIGHEST
    back_r = jnp.einsum("...cd,da->...ca", spec_r, cos_a, precision=high) - jnp.einsum(
        "...cd,da->...ca", spec_i, sin_a, precision=high
    )
    back_i = jnp.einsum("...cd,da->...ca", spec_i, cos_a, precision=high) + jnp.einsum(
        "...cd,da->...ca", spec_r, sin_a, precision=high
    )
    turn_r = back_r * twist_r - back_i * twist_s
    turn_i = back_i * twist_r + back_r * twist_s
    whole = jnp.einsum("bc,...ca->...ba", cos_b, turn_r, precision=high) - jnp.einsum(
        "bc,...ca->...ba", sin_b, turn_i, precision=high
    )
    return whole / (side_b * side_a)


def convolve(fields, filt, tables):
    side_b, side_a = (tables[0], tables[1])
    length = side_b * side_a
    chans = fields.shape[1]
    stacked = jnp.concatenate([fields[0:1], filt[None], fields[1:]], axis=0).astype(jnp.float32)
    spec_r, spec_i = forward_dft(stacked.reshape(8, chans, side_b, side_a), tables)
    prod_r = spec_r[0] * spec_r[1] - spec_i[0] * spec_i[1]
    prod_i = spec_r[0] * spec_i[1] + spec_i[0] * spec_r[1]
    key_r, key_i = (spec_r[2:5], spec_i[2:5])
    val_r, val_i = (spec_r[5:8], spec_i[5:8])
    k_one_r, k_one_i = (jnp.roll(key_r, -1, axis=0), jnp.roll(key_i, -1, axis=0))
    k_two_r, k_two_i = (jnp.roll(key_r, -2, axis=0), jnp.roll(key_i, -2, axis=0))
    v_one_r, v_one_i = (jnp.roll(val_r, -1, axis=0), jnp.roll(val_i, -1, axis=0))
    v_two_r, v_two_i = (jnp.roll(val_r, -2, axis=0), jnp.roll(val_i, -2, axis=0))
    cross_r = k_one_r * v_two_r - k_one_i * v_two_i - (k_two_r * v_one_r - k_two_i * v_one_i)
    cross_i = k_one_r * v_two_i + k_one_i * v_two_r - (k_two_r * v_one_i + k_two_i * v_one_r)
    all_r = jnp.concatenate([prod_r[None], cross_r], axis=0)
    all_i = jnp.concatenate([prod_i[None], cross_i], axis=0)
    result = inverse_dft(all_r, all_i, tables).reshape(4, chans, length)
    inv_root = 1.0 / math.sqrt(length)
    scale = jnp.array([1.0, inv_root, inv_root, inv_root], dtype=jnp.float32)
    return (result * scale[:, None, None]).astype(jnp.bfloat16)


def plain_device(
    scalars,
    vectors,
    w_qkw_s,
    w_qkw_v,
    w_out_s,
    w_out_v,
    w_up,
    w_down,
    w_mix,
    w_gate,
    gains,
    pe_w1,
    pe_w2,
    pe_w3,
    rates,
):
    chans = scalars.shape[0]
    tok_local = scalars.shape[1]
    shards = lax.axis_size("seq")
    rank = lax.axis_index("seq")
    length = tok_local * shards
    depth = w_qkw_s.shape[0]
    tables = make_tables(length)
    local_pos = rank * tok_local + jnp.arange(tok_local, dtype=jnp.int32)
    made = jnp.stack(
        [
            filter_values(local_pos, length, pe_w1[layer], pe_w2[layer], pe_w3[layer], rates[layer])
            for layer in range(depth)
        ],
        axis=0,
    )
    filters = lax.all_to_all(made, "seq", split_axis=1, concat_axis=2, tiled=True)
    state_s = scalars.astype(jnp.float32)
    state_v = vectors.astype(jnp.float32)
    for layer in range(depth):
        normed_s = scalar_norm(state_s, gains[layer, 0]).astype(jnp.bfloat16)
        normed_v = vector_norm(state_v, gains[layer, 1]).astype(jnp.bfloat16)
        proj_s = jnp.dot(w_qkw_s[layer], normed_s, preferred_element_type=jnp.float32)
        query_s = proj_s[:chans].astype(jnp.bfloat16)
        signal_s = (proj_s[chans : 2 * chans] * proj_s[2 * chans :]).astype(jnp.bfloat16)
        proj_v = jnp.einsum(
            "oc,jct->jot", w_qkw_v[layer], normed_v, preferred_element_type=jnp.float32
        ).astype(jnp.bfloat16)
        query_v = proj_v[:, :chans]
        outgoing = jnp.concatenate(
            [signal_s[None], proj_v[:, chans : 2 * chans], proj_v[:, 2 * chans :]], axis=0
        )
        regrouped = lax.all_to_all(outgoing, "seq", split_axis=1, concat_axis=2, tiled=True)
        convolved = convolve(regrouped, filters[layer], tables)
        returned = lax.all_to_all(convolved, "seq", split_axis=2, concat_axis=1, tiled=True)
        conv_f = returned.astype(jnp.float32)
        qs_f = query_s.astype(jnp.float32)
        out_s = (
            qs_f * conv_f[0] + jnp.sum(query_v.astype(jnp.float32) * conv_f[1:], axis=0)
        ).astype(jnp.bfloat16)
        out_v = (qs_f[None] * conv_f[1:]).astype(jnp.bfloat16)
        state_s = state_s + jnp.dot(w_out_s[layer], out_s, preferred_element_type=jnp.float32)
        state_v = state_v + jnp.einsum(
            "oc,jct->jot", w_out_v[layer], out_v, preferred_element_type=jnp.float32
        )
        mlp_s = scalar_norm(state_s, gains[layer, 2]).astype(jnp.bfloat16)
        mlp_v = vector_norm(state_v, gains[layer, 3]).astype(jnp.bfloat16)
        hidden = jax.nn.gelu(
            jnp.dot(w_up[layer], mlp_s, preferred_element_type=jnp.float32)
        ).astype(jnp.bfloat16)
        gate = jax.nn.sigmoid(jnp.dot(w_gate[layer], mlp_s, preferred_element_type=jnp.float32))
        state_s = state_s + jnp.dot(w_down[layer], hidden, preferred_element_type=jnp.float32)
        state_v = (
            state_v
            + jnp.einsum("oc,jct->jot", w_mix[layer], mlp_v, preferred_element_type=jnp.float32)
            * gate[None]
        )
    return (state_s.astype(jnp.bfloat16), state_v.astype(jnp.bfloat16))


def reduced_sine(angle):
    turns = jnp.floor(angle * (1.0 / math.pi) + 0.5)
    rest = angle - turns * 3.140625
    rest = rest - turns * 9.67502593994140625e-4
    rest = rest - turns * 1.509957990978376432e-7
    half = turns * 0.5
    sign = 1.0 - 4.0 * (half - jnp.floor(half))
    sq = rest * rest
    poly = -2.5052108e-8
    poly = poly * sq + 2.7557319e-6
    poly = poly * sq - 1.9841270e-4
    poly = poly * sq + 8.3333333e-3
    poly = poly * sq - 1.6666667e-1
    return sign * (rest + rest * sq * poly)


def part_sum(one, two):
    if one is None:
        return two
    if two is None:
        return one
    return one + two


def part_diff(one, two):
    if two is None:
        return one
    if one is None:
        return -two
    return one - two


def turn(value, step, count):
    step = step % count
    real, imag = value
    if step == 0:
        return value
    if 4 * step == count:
        return (None if imag is None else -imag, real)
    if 4 * step == 3 * count:
        return (imag, None if real is None else -real)
    cos, sin = (math.cos(2 * math.pi * step / count), math.sin(2 * math.pi * step / count))
    if imag is None:
        return (real * cos, real * sin)
    if real is None:
        return (imag * -sin, imag * cos)
    return (real * cos - imag * sin, imag * cos + real * sin)


def real_fft(fields):
    count = len(fields)
    if count == 1:
        return [(fields[0], None)]
    if count == 2:
        return [(fields[0] + fields[1], None), (fields[0] - fields[1], None)]
    even, odd = (real_fft(fields[0::2]), real_fft(fields[1::2]))
    out = [None] * (count // 2 + 1)
    for k in range(count // 4 + 1):
        spun = turn(odd[k], -k, count)
        out[k] = (part_sum(even[k][0], spun[0]), part_sum(even[k][1], spun[1]))
        back = (part_diff(even[k][0], spun[0]), part_diff(spun[1], even[k][1]))
        if count // 2 - k != k:
            out[count // 2 - k] = back
    return out


def inverse_real_fft(spec, count):
    if count == 1:
        return [spec[0][0]]
    if count == 2:
        return [spec[0][0] + spec[1][0], spec[0][0] - spec[1][0]]
    even, odd = ([], [])
    for k in range(count // 4 + 1):
        one, two = (spec[k], spec[count // 2 - k])
        if 4 * k == count:
            even.append((one[0] * 2.0, None))
            odd.append((one[1] * -2.0, None))
            continue
        even.append((part_sum(one[0], two[0]), part_diff(one[1], two[1])))
        diff = (part_diff(one[0], two[0]), part_sum(one[1], two[1]))
        odd.append(turn(diff, k, count))
    out = [None] * count
    out[0::2] = inverse_real_fft(even, count // 2)
    out[1::2] = inverse_real_fft(odd, count // 2)
    return out


def local_tables(shards, tok_local):
    length = shards * tok_local
    freq = np.arange(shards // 2 + 1)[:, None, None] + shards * np.arange(tok_local)[None, None, :]
    angle = (np.arange(tok_local)[None, :, None] * freq % length) * (2.0 * np.pi / length)
    cos, sin = (np.cos(angle), np.sin(angle))
    fore = np.concatenate(
        [np.concatenate([cos, -sin], axis=2), np.concatenate([sin, cos], axis=2)], axis=1
    )
    return jnp.asarray(fore, jnp.float32)


def layers_kernel(shards, count, *refs):
    outside, refs = (refs[:count], refs[count:])
    scalars_out, vectors_out, *refs = refs
    inside, refs = (refs[:count], refs[count:])
    load_sem, state_s, state_v, columns, ready_s, query_s, query_v, *refs = refs
    fore, made_f, sent_x, got_x, sent_y, got_y, mid, spec, inv, send_sem, recv_sem = refs
    scalars, vectors, w_qkw_s, w_qkw_v, w_out_s, w_out_v, w_up, w_down, w_mix, w_gate = inside[:10]
    gains, pe_w1, pe_w2, pe_w3, rates, fore_wide = inside[10:]
    loads = [
        pltpu.make_async_copy(outside[i], inside[i], load_sem.at[i]) for i in range(count)
    ]
    for i in (1, 3, 10, 0, 2, 11, 12, 13, 14, 15, 5, 8, 4, 6, 9, 7):
        loads[i].start()

    def need(*places):
        for i in places:
            loads[i].wait()

    grp = lax.axis_index("grp")
    me = lax.axis_index("seq")
    chans, tok = scalars.shape
    own = chans // shards
    length = shards * tok
    depth = w_qkw_s.shape[0]
    half = shards // 2 + 1
    f32, bf16 = (jnp.float32, jnp.bfloat16)
    mesh_id = pl.DeviceIdType.MESH

    barrier = pltpu.get_barrier_semaphore()

    def greet(step, carry):
        peer = lax.rem(me + step, shards)
        pl.semaphore_signal(barrier, inc=1, device_id=(grp, peer), device_id_type=mesh_id)
        return carry

    lax.fori_loop(1, shards, greet, 0)

    def copy_of(kind, src, dst, peer):
        return pltpu.make_async_remote_copy(
            src_ref=src,
            dst_ref=dst,
            send_sem=send_sem.at[kind],
            recv_sem=recv_sem.at[kind],
            device_id=(grp, peer),
            device_id_type=mesh_id,
        )

    def send(kind, src, dst, rows):
        def body(turn, carry):
            side = lax.rem(turn, 2)
            step = shards // 2 + (1 - 2 * side) * ((turn + 1) // 2)
            peer = lax.rem(me + step, shards)
            copy_of(kind, src.at[peer, rows], dst.at[me, rows], peer).start()
            return carry

        lax.fori_loop(0, shards - 1, body, 0)
        dst[pl.ds(me, 1), rows] = src[pl.ds(me, 1), rows]

    def all_of(kind, ref, rows):
        blocks = ref.at[pl.ds(0, shards - 1), rows]
        return copy_of(kind, blocks, blocks, lax.rem(me + 1, shards))

    def receive(kind, dst, rows):
        all_of(kind, dst, rows).wait_recv()

    def sent(kind, src, rows):
        all_of(kind, src, rows).wait_send()

    def column(row):
        return jnp.broadcast_to(row, (tok, chans)).T

    def normed_scalar(field, gain):
        return (
            field * lax.rsqrt(jnp.mean(field * field, axis=0, keepdims=True) + 1e-05) * gain
        ).astype(bf16)

    def normed_vector(fields, gain):
        total = sum(jnp.sum(field * field, axis=0, keepdims=True) for field in fields)
        scale = lax.rsqrt(total * (1.0 / (3 * chans)) + 1e-05)
        return jnp.concatenate([(field * scale * gain).astype(bf16) for field in fields], axis=1)

    def make_filter(layer):
        freqs = pe_w1.shape[1] // 2
        high = lax.Precision.HIGHEST
        lhs_rows = (((0,), (0,)), ((), ()))
        pick = (
            lax.broadcasted_iota(jnp.int32, (own, chans), 1)
            == me * own + lax.broadcasted_iota(jnp.int32, (own, chans), 0)
        ).astype(f32)
        rate = jnp.sum(pick * rates[layer : layer + 1, :], axis=1, keepdims=True)
        third = lax.dot_general(
            pick, pe_w3[layer], (((1,), (1,)), ((), ())), precision=high, preferred_element_type=f32
        )
        span = tok * math.gcd(4, shards)
        for start in range(0, length, span):
            row = lax.broadcasted_iota(jnp.int32, (2 * freqs, span), 0)
            pos = start + lax.broadcasted_iota(jnp.int32, (2 * freqs, span), 1)
            is_cos = row < freqs
            turns = (jnp.where(is_cos, row + 1, row + 1 - freqs) * pos).astype(f32)
            turns = turns + jnp.where(is_cos, length / 4.0, 0.0)
            turns = turns - length * jnp.floor(turns * (1.0 / length))
            feats = reduced_sine(turns * (2.0 * math.pi / length))
            one = reduced_sine(
                lax.dot_general(
                    pe_w1[layer], feats, lhs_rows, precision=high, preferred_element_type=f32
                )
            )
            two = reduced_sine(
                jnp.dot(pe_w2[layer], one, precision=high, preferred_element_type=f32)
            )
            raw = jnp.dot(third, two, precision=high, preferred_element_type=f32)
            place = (start + lax.broadcasted_iota(jnp.int32, (own, span), 1)).astype(f32)
            made = raw * jnp.exp(-rate * place * (1.0 / length)) * (1.0 / math.sqrt(length))
            for r in range(span // tok):
                made_f[start // tok + r] = made[:, r * tok : (r + 1) * tok].astype(bf16)

    def spread(fields, row):
        spec = real_fft(fields)
        for k in range(half):
            real, imag = spec[k]
            mid[k, row : row + own, 0:tok] = real.astype(bf16)
            if imag is None:
                imag = jnp.zeros_like(real)
            mid[k, row : row + own, tok : 2 * tok] = imag.astype(bf16)

    def gather_back(layer, signal, scale):
        spec = []
        for k in range(half):
            imag = None if k in (0, half - 1) else inv[k, signal * own : (signal + 1) * own, tok : 2 * tok]
            spec.append((inv[k, signal * own : (signal + 1) * own, 0:tok], imag))
        out = inverse_real_fft(spec, shards)
        for r in range(shards):
            sent_y[layer, r, signal * own : (signal + 1) * own, :] = (out[r] * scale).astype(bf16)

    def incoming(ref, row):
        return [ref[r, row : row + own, :].astype(f32) for r in range(shards)]

    def times(one, two):
        return (one[0] * two[0] - one[1] * two[1], one[0] * two[1] + one[1] * two[0])

    def undo(spec, k):
        return lax.dot_general(
            spec, fore[k], (((1,), (1,)), ((), ())), preferred_element_type=f32
        )

    need(1)
    state_v[...] = vectors[...].astype(f32)
    x_rows = (pl.ds(0, 4 * own), pl.ds(4 * own, 2 * own), pl.ds(6 * own, own))
    y_rows = (pl.ds(0, own), pl.ds(own, 2 * own), pl.ds(3 * own, own))
    key_slot, val_slot = ((4, 0, 1), (5, 2, 3))

    def part(k, slot):
        return (
            spec[k, slot * own : (slot + 1) * own, :tok],
            spec[k, slot * own : (slot + 1) * own, tok:],
        )

    def cross(k, j):
        one, two = ((j + 1) % 3, (j + 2) % 3)
        plus = times(part(k, key_slot[one]), part(k, val_slot[two]))
        minus = times(part(k, key_slot[two]), part(k, val_slot[one]))
        return jnp.concatenate([plus[0] - minus[0], plus[1] - minus[1]], axis=1)

    def transform(first, last):
        for k in range(half):
            spec[k, first * own : last * own, :] = jnp.dot(
                mid[k, first * own : last * own, :], fore[k], preferred_element_type=f32
            )

    def finish_scalar(layer):
        wide = jnp.dot(w_up[layer], ready_s[...], preferred_element_type=f32)
        hidden = jax.nn.gelu(wide).astype(bf16)
        return state_s[...] + jnp.dot(w_down[layer], hidden, preferred_element_type=f32)

    for layer in range(depth):
        base = 6 * layer
        fields = [state_v[j] for j in range(3)]
        if layer == 0:
            need(10, 3)
            columns[1] = column(gains[0, 1:2, :])
        vn = normed_vector(fields, columns[4 * layer + 1])
        w_kw = w_qkw_v[layer, chans:, :]
        pv = jnp.dot(w_kw, vn[:, tok:], preferred_element_type=f32).astype(bf16)
        for slot in range(4):
            rows = slice((slot // 2) * chans, (slot // 2 + 1) * chans)
            cols = slice((slot % 2) * tok, (slot % 2 + 1) * tok)
            sent_x[layer, :, slot * own : (slot + 1) * own, :] = pv[rows, cols].reshape(
                shards, own, tok
            )
        if layer == 0:
            pl.semaphore_wait(barrier, shards - 1)
        send(base, sent_x.at[layer], got_x.at[layer], x_rows[0])
        pv = jnp.dot(w_kw, vn[:, :tok], preferred_element_type=f32).astype(bf16)
        for slot in range(2):
            rows = slice(slot * chans, (slot + 1) * chans)
            sent_x[layer, :, (4 + slot) * own : (5 + slot) * own, :] = pv[rows].reshape(
                shards, own, tok
            )
        send(base + 1, sent_x.at[layer], got_x.at[layer], x_rows[1])
        if layer == 0:
            need(0, 2)
            state_s[...] = scalars[...].astype(f32)
            columns[0] = column(gains[0, 0:1, :])
        else:
            state_s[...] = finish_scalar(layer - 1)
        sn = normed_scalar(state_s[...], columns[4 * layer])
        ps = jnp.dot(w_qkw_s[layer, chans:, :], sn, preferred_element_type=f32)
        sent_x[layer, :, 6 * own : 7 * own, :] = (
            (ps[:chans] * ps[chans:]).astype(bf16).reshape(shards, own, tok)
        )
        send(base + 2, sent_x.at[layer], got_x.at[layer], x_rows[2])
        query_s[...] = jnp.dot(w_qkw_s[layer, :chans, :], sn, preferred_element_type=f32).astype(bf16)
        query_v[...] = jnp.dot(w_qkw_v[layer, :chans, :], vn, preferred_element_type=f32).astype(bf16)
        if layer == 0:
            for place in range(2, 4 * depth):
                columns[place] = column(gains[place // 4, place % 4 : place % 4 + 1, :])
            need(11, 12, 13, 14)
        make_filter(layer)
        spread(incoming(made_f, 0), 7 * own)
        if layer == 0:
            need(15)
            fore[...] = fore_wide[...].astype(bf16)

        receive(base, got_x.at[layer], x_rows[0])
        for slot in range(4):
            spread(incoming(got_x.at[layer], slot * own), slot * own)
        transform(0, 4)
        for k in range(half):
            inv[k, :own, :] = undo(cross(k, 0).astype(bf16), k)
        gather_back(layer, 0, 1.0 / (length * math.sqrt(length)))
        send(base + 3, sent_y.at[layer], got_y.at[layer], y_rows[0])

        receive(base + 1, got_x.at[layer], x_rows[1])
        for slot in range(4, 6):
            spread(incoming(got_x.at[layer], slot * own), slot * own)
        transform(4, 6)
        for k in range(half):
            both = jnp.concatenate([cross(k, 1), cross(k, 2)], axis=0)
            inv[k, own : 3 * own, :] = undo(both.astype(bf16), k)
        for signal in range(1, 3):
            gather_back(layer, signal, 1.0 / (length * math.sqrt(length)))
        send(base + 4, sent_y.at[layer], got_y.at[layer], y_rows[1])

        receive(base + 2, got_x.at[layer], x_rows[2])
        spread(incoming(got_x.at[layer], 6 * own), 6 * own)
        transform(6, 8)
        for k in range(half):
            prod = times(part(k, 6), part(k, 7))
            inv[k, 3 * own :, :] = undo(jnp.concatenate(prod, axis=1).astype(bf16), k)
        gather_back(layer, 3, 1.0 / length)
        send(base + 5, sent_y.at[layer], got_y.at[layer], y_rows[2])

        if layer == 0:
            need(5, 8, 4, 6, 9, 7)
        qs = query_s[...].astype(f32)
        out_v = []
        mixed = None
        for j in range(3):
            if j < 2:
                receive(base + 3 + j, got_y.at[layer], y_rows[j])
            field = got_y[layer, :, j * own : (j + 1) * own, :].reshape(chans, tok).astype(f32)
            term = query_v[:, j * tok : (j + 1) * tok].astype(f32) * field
            mixed = term if mixed is None else mixed + term
            out_v.append((qs * field).astype(bf16))
        moved = jnp.dot(w_out_v[layer], jnp.concatenate(out_v, axis=1), preferred_element_type=f32)
        fields = [state_v[j] + moved[:, j * tok : (j + 1) * tok] for j in range(3)]
        vm = normed_vector(fields, columns[4 * layer + 3])
        mix = jnp.dot(w_mix[layer], vm, preferred_element_type=f32)
        receive(base + 5, got_y.at[layer], y_rows[2])
        field = got_y[layer, :, 3 * own : 4 * own, :].reshape(chans, tok).astype(f32)
        out_s = (qs * field + mixed).astype(bf16)
        now_s = state_s[...] + jnp.dot(w_out_s[layer], out_s, preferred_element_type=f32)
        sm = normed_scalar(now_s, columns[4 * layer + 2])
        gate = jax.nn.sigmoid(jnp.dot(w_gate[layer], sm, preferred_element_type=f32))
        now_v = [fields[j] + mix[:, j * tok : (j + 1) * tok] * gate for j in range(3)]
        ready_s[...] = sm
        state_s[...] = now_s
        if layer + 1 < depth:
            for j in range(3):
                state_v[j] = now_v[j]
        else:
            for j in range(3):
                vectors_out[j] = now_v[j].astype(bf16)
            scalars_out[...] = finish_scalar(layer).astype(bf16)
    for layer in range(depth):
        for i in range(3):
            sent(6 * layer + i, sent_x.at[layer], x_rows[i])
            sent(6 * layer + 3 + i, sent_y.at[layer], y_rows[i])


def place_results(scalars, vectors, scalars_out, vectors_out):
    vectors_out[...] = vectors[...]
    scalars_out[...] = scalars[...]


def per_device(*arrays):
    scalars, vectors, w_qkw_s = arrays[:3]
    chans, tok = scalars.shape
    shards = lax.axis_size("seq")
    depth = w_qkw_s.shape[0]
    own = chans // shards
    if tok % 128 or own % 16 or chans % shards or shards & (shards - 1) or shards < 4:
        return plain_device(*arrays)
    half = shards // 2 + 1
    f32, bf16 = (jnp.float32, jnp.bfloat16)
    arrays = list(arrays)
    arrays[11] = jnp.swapaxes(arrays[11], 1, 2)
    arrays[13] = jnp.swapaxes(arrays[13], 1, 2)
    arrays.append(local_tables(shards, tok))
    count = len(arrays)
    whole = pl.BlockSpec(memory_space=pltpu.VMEM)
    made = pl.pallas_call(
        functools.partial(layers_kernel, shards, count),
        out_shape=(
            jax.ShapeDtypeStruct(scalars.shape, bf16),
            jax.ShapeDtypeStruct(vectors.shape, bf16),
        ),
        in_specs=[pl.BlockSpec(memory_space=pltpu.HBM)] * count,
        out_specs=(whole, whole),
        scratch_shapes=[pltpu.VMEM(array.shape, array.dtype) for array in arrays]
        + [
            pltpu.SemaphoreType.DMA((count,)),
            pltpu.VMEM((chans, tok), f32),
            pltpu.VMEM((3, chans, tok), f32),
            pltpu.VMEM((4 * depth, chans, tok), f32),
            pltpu.VMEM((chans, tok), bf16),
            pltpu.VMEM((chans, tok), bf16),
            pltpu.VMEM((chans, 3 * tok), bf16),
            pltpu.VMEM((half, 2 * tok, 2 * tok), bf16),
            pltpu.VMEM((shards, own, tok), bf16),
            pltpu.VMEM((depth, shards, 7 * own, tok), bf16),
            pltpu.VMEM((depth, shards, 7 * own, tok), bf16),
            pltpu.VMEM((depth, shards, 4 * own, tok), bf16),
            pltpu.VMEM((depth, shards, 4 * own, tok), bf16),
            pltpu.VMEM((half, 8 * own, 2 * tok), bf16),
            pltpu.VMEM((half, 8 * own, 2 * tok), f32),
            pltpu.VMEM((half, 4 * own, 2 * tok), f32),
            pltpu.SemaphoreType.DMA((6 * depth,)),
            pltpu.SemaphoreType.DMA((6 * depth,)),
        ],
        compiler_params=pltpu.CompilerParams(
            collective_id=0, has_side_effects=True, vmem_limit_bytes=63 * 1024 * 1024
        ),
        name="hyena_layers",
    )(*arrays)
    return pl.pallas_call(
        place_results,
        out_shape=tuple(jax.ShapeDtypeStruct(one.shape, one.dtype) for one in made),
        in_specs=[whole, whole],
        out_specs=(whole, whole),
        compiler_params=pltpu.CompilerParams(vmem_limit_bytes=63 * 1024 * 1024),
        name="place_results",
    )(*made)


def solution(mesh):
    in_specs = (
        P(None, ("grp", "seq")),
        P(None, None, ("grp", "seq")),
        P(),
        P(),
        P(),
        P(),
        P(),
        P(),
        P(),
        P(),
        P(),
        P(),
        P(),
        P(),
        P(),
    )
    out_specs = (P(None, ("grp", "seq")), P(None, None, ("grp", "seq")))
    return jax.shard_map(
        per_device, mesh=mesh, in_specs=in_specs, out_specs=out_specs, check_vma=False
    )
```
